32 devices in a mesh: dp: 4 (over y, x), shard: 8 (over z, core).
Axes of the slice: x: 2, y: 2, z: 4, core: 2. Of those that a mesh axis runs over, the one named last changes fastest.
Arguments:
- inputs: bfloat16 [2, 1024, 8192], P(None, 'dp', 'shard'), may hold values from -6 to 6
- key_panel: bfloat16 [8192, 4096], P('dp', 'shard'), may hold values from -0.0625 to 0.0625
- value_panel: bfloat16 [8192, 4096], P('dp', 'shard'), may hold values from -0.0625 to 0.0625
- short_filters: float32 [2, 4096, 7], P(None, 'shard'), may hold values from -2 to 2
- medium_filters: float32 [256, 128], P('shard'), may hold values from -0.5 to 0.5
- lengths: int32 [2], replicated, may hold values from 512 to 1024, as said below
- cotangent: bfloat16 [2, 1024, 4096], P(None, 'dp', 'shard'), may hold values from -0.099609375 to 0.099609375
Outputs:
- mixed: bfloat16 [2, 1024, 4096], P(None, 'dp', 'shard')
- key_grad: bfloat16 [8192, 4096], P('dp', 'shard')
- value_grad: bfloat16 [8192, 4096], P('dp', 'shard')
- short_grad: float32 [2, 4096, 7], P(None, 'shard')
- medium_grad: float32 [256, 128], P('shard')
The draws below stay inside these ranges and needn't reach their ends.
Inputs may be any that keep to these rules, and one draw needn't show every extreme that they name: `lengths`: each length is a multiple of 16; one window in every draw has the full length 1024, the others are shorter.
All inputs are finite; a program needn't handle non-finite values.
Results may differ from the reference program's by a relative error of at most 0.014.
Values may be sent and summed in bfloat16 or wider, within the bound.
A program may use at most 128 MiB of HBM per device.

```python
import jax
import jax.numpy as jnp
from jax import lax

D = 8192
SHORT = 7
MEDIUM = 128
GROUP = 16
C = 4096
SEQS = 2
LEN_DEV = 256
LEN = 1024
GROUPS = 256
N_DP = 4


def draw_lengths(key, part):
    first_key, second_key = jax.random.split(key)
    steps_all = LEN // 16
    drawn = jax.random.randint(first_key, (SEQS,), steps_all // 2, steps_all) * 16
    longest = jax.random.randint(second_key, (), 0, SEQS)
    chosen = jnp.arange(SEQS) == longest
    return jnp.where(chosen, LEN, drawn).astype(jnp.int32)


def levels(rng, extent, cuts, low, top_value):
    def one(position, parts):
        heights = jax.random.uniform(jax.random.fold_in(jax.random.fold_in(rng, 6), position), (parts,), jnp.float32, low / len(cuts), top_value / len(cuts))
        return jnp.repeat(jnp.exp(heights), extent[position] // parts).reshape((-1,) + (1,) * (len(extent) - position - 1))

    factor_of = one(*cuts[0])
    for cut in cuts[1:]:
        factor_of = factor_of * one(*cut)
    return factor_of


def noise(stream_key, extent, spread, reach, cuts=(), kind=jnp.bfloat16):
    values = jax.random.normal(stream_key, extent, jnp.float32) * spread
    if len(cuts) > 0:
        values = levels(stream_key, extent, cuts, -0.22, 0.18) * values
    return jnp.clip(values, min=-reach, max=reach).astype(kind)


def setup_inputs(seed: int = 0) -> dict:
    seeds = jax.random.split(jax.random.key(seed), 8)
    return {
        "inputs": noise(seeds[0], (SEQS, LEN, D), 1.0, 6.0, ((1, 4), (2, 8))),
        "key_panel": noise(seeds[1], (D, C), D ** -0.5, 0.0625, ((0, 4), (1, 8))),
        "value_panel": noise(seeds[2], (D, C), D ** -0.5, 0.0625, ((0, 4), (1, 8))),
        "short_filters": noise(seeds[3], (2, C, SHORT), 0.38, 2.0, ((1, 8),), jnp.float32),
        "medium_filters": noise(seeds[4], (GROUPS, MEDIUM), 0.088, 0.5, ((0, 8),), jnp.float32),
        "lengths": draw_lengths(jax.random.fold_in(seeds[7], 71), 0),
        "cotangent": noise(seeds[6], (SEQS, LEN, C), 0.015625, 0.099609375, ((1, 4), (2, 8))),
    }


def rounded(values):
    return lax.optimization_barrier(values.astype(jnp.bfloat16)).astype(jnp.float32)

def delay(values, steps):
    count = values.shape[1]
    return jnp.pad(values, ((0, 0), (steps, 0), (0, 0)))[:, :count]

def advance(values, steps):
    return jnp.pad(values, ((0, 0), (0, steps), (0, 0)))[:, steps:]

def short_forward(values, filters):
    total = jnp.zeros(values.shape, jnp.float32)
    for tap in range(SHORT):
        total = total + filters[:, tap] * delay(values, tap)
    return total

def short_backward(grads, filters):
    total = jnp.zeros(grads.shape, jnp.float32)
    for tap in range(SHORT):
        total = total + filters[:, tap] * advance(grads, tap)
    return total

def short_filter_grad(grads, values):
    return jnp.stack([lax.optimization_barrier(jnp.sum(grads * delay(values, tap), axis=(0, 1))) for tap in range(SHORT)], axis=-1)

def medium_forward(product, per_channel):
    padded = jnp.pad(product, ((0, 0), (MEDIUM - 1, 0), (0, 0)))

    def step(tap, total):
        column = lax.dynamic_slice_in_dim(per_channel, tap, 1, 1)[:, 0]
        return total + column * lax.dynamic_slice_in_dim(padded, MEDIUM - 1 - tap, LEN, 1)
    return lax.fori_loop(0, MEDIUM, step, jnp.zeros(product.shape, jnp.float32))

def medium_backward(upstream, per_channel):
    padded = jnp.pad(upstream, ((0, 0), (0, MEDIUM - 1), (0, 0)))

    def step(tap, total):
        column = lax.dynamic_slice_in_dim(per_channel, tap, 1, 1)[:, 0]
        return total + column * lax.dynamic_slice_in_dim(padded, tap, LEN, 1)
    return lax.fori_loop(0, MEDIUM, step, jnp.zeros(upstream.shape, jnp.float32))

def medium_filter_grad(upstream, product):
    padded = jnp.pad(product, ((0, 0), (MEDIUM - 1, 0), (0, 0)))

    def step(carry, tap):
        shifted = lax.dynamic_slice_in_dim(padded, MEDIUM - 1 - tap, LEN, 1)
        return (carry, lax.optimization_barrier(jnp.sum(upstream * shifted, axis=(0, 1))))
    _, sums = lax.scan(step, jnp.zeros((), jnp.float32), jnp.arange(MEDIUM))
    return sums.T.reshape(GROUPS, GROUP, MEDIUM).sum(axis=1)

def reference(inputs, key_panel, value_panel, short_filters, medium_filters, lengths, cotangent):
    flat = inputs.reshape(SEQS * LEN, D)
    keys = rounded(jnp.dot(flat, key_panel, preferred_element_type=jnp.float32)).reshape(SEQS, LEN, C)
    values = rounded(jnp.dot(flat, value_panel, preferred_element_type=jnp.float32)).reshape(SEQS, LEN, C)
    smooth_keys = short_forward(keys, short_filters[0])
    smooth_values = short_forward(values, short_filters[1])
    product = rounded(smooth_keys * smooth_values)
    per_channel = jnp.repeat(medium_filters, GROUP, axis=0)
    response = medium_forward(product, per_channel)
    positions = jnp.arange(LEN)
    live = (positions[None, :] < lengths[:, None]).astype(jnp.float32)[:, :, None]
    mixed = (response * live).astype(jnp.bfloat16)
    upstream = cotangent.astype(jnp.float32) * live
    product_grad = medium_backward(upstream, per_channel)
    medium_grad = medium_filter_grad(upstream, product)
    key_smooth_grad = product_grad * smooth_values
    value_smooth_grad = product_grad * smooth_keys
    short_grad = jnp.stack([short_filter_grad(key_smooth_grad, keys), short_filter_grad(value_smooth_grad, values)])
    key_act = short_backward(key_smooth_grad, short_filters[0]).astype(jnp.bfloat16)
    value_act = short_backward(value_smooth_grad, short_filters[1]).astype(jnp.bfloat16)
    both_grads = jnp.concatenate([key_act, value_act], axis=2)

    def accumulate(index, total):
        begin = index * LEN_DEV
        block = lax.dynamic_slice_in_dim(inputs, begin, LEN_DEV, 1).reshape(SEQS * LEN_DEV, D)
        grad_block = lax.dynamic_slice_in_dim(both_grads, begin, LEN_DEV, 1).reshape(SEQS * LEN_DEV, 2 * C)
        partial_sum = lax.dot_general(block, grad_block, (((0,), (0,)), ((), ())), preferred_element_type=jnp.float32)
        return total + rounded(partial_sum)
    summed = lax.fori_loop(0, N_DP, accumulate, jnp.zeros((D, 2 * C), jnp.float32))
    key_grad = summed[:, :C].astype(jnp.bfloat16)
    value_grad = summed[:, C:].astype(jnp.bfloat16)
    return (mixed, key_grad, value_grad, short_grad, medium_grad)
```

```python
import functools

import jax
import jax.numpy as jnp
from jax import lax
from jax.experimental import pallas as pl
from jax.experimental.pallas import tpu as pltpu
from jax.sharding import PartitionSpec as P

BLOCK = 128


def shifted(value, axis, steps):
    count = lax.axis_size(axis)
    first, last = (max(0, -steps), min(count, count - steps))
    return lax.ppermute(value, axis, [(source, source + steps) for source in range(first, last)])


def band(filters, count):
    groups, taps = filters.shape
    width = count + taps - 1
    padded = jnp.concatenate([filters, jnp.zeros((groups, count), jnp.float32)], axis=1)
    tiled = jnp.tile(padded, (1, count))[:, : count * width]
    return tiled.reshape(groups, count, width)


def band_sums(correlation, count, taps):
    groups, _, width = correlation.shape
    flat = correlation.reshape(groups, count * width)
    padded = jnp.concatenate([flat, jnp.zeros((groups, count), jnp.float32)], axis=1)
    skewed = padded.reshape(groups, count, width + 1)
    return jnp.sum(skewed, axis=1)[:, :taps][:, ::-1]


def short_taps(extended, filters, count):
    width = filters.shape[-1]
    total = jnp.zeros(extended.shape[:2] + (count, extended.shape[3]), jnp.float32)
    for tap in range(width):
        begin = width - 1 - tap
        total = total + filters[:, None, None, :, tap] * extended[
            :, :, begin : begin + count
        ].astype(jnp.float32)
    return total


def short_ahead(extended, filters, count):
    width = filters.shape[-1]
    total = jnp.zeros(extended.shape[:2] + (count, extended.shape[3]), jnp.float32)
    for tap in range(width):
        total = total + filters[:, None, None, :, tap] * extended[:, :, tap : tap + count]
    return total


def filter_terms(grads, extended, count, width):
    columns = []
    for tap in range(width):
        begin = width - 1 - tap
        columns.append(
            jnp.sum(grads * extended[:, :, begin : begin + count].astype(jnp.float32), axis=(1, 2))
        )
    return jnp.stack(columns, axis=-1)


def by_positions(inputs, key_panel, value_panel, short_filters, medium_filters, lengths, cotangent):
    seqs, count, local_width = inputs.shape
    channels = key_panel.shape[1]
    groups, taps = medium_filters.shape
    group_size = channels // groups
    short_width = short_filters.shape[-1]
    span = count + taps - 1
    gathered = (
        lax.all_gather(key_panel, "dp", axis=0, tiled=True),
        lax.all_gather(value_panel, "dp", axis=0, tiled=True),
    )
    panels = jnp.concatenate([gathered[0], gathered[1]], axis=1)
    features = lax.all_gather(inputs, "shard", axis=2, tiled=True)
    projected = jnp.dot(
        features.reshape(seqs * count, -1), panels, preferred_element_type=jnp.float32
    )
    paired = projected.astype(jnp.bfloat16).reshape(seqs, count, 2, channels).transpose(2, 0, 1, 3)
    head_rows = shifted(paired[:, :, count - (short_width - 1) :], "dp", 1)
    extended = jnp.concatenate([head_rows, paired], axis=2)
    smoothed = short_taps(extended, short_filters, count)
    product = (smoothed[0] * smoothed[1]).astype(jnp.bfloat16)
    before = shifted(product[:, count - (taps - 1) :], "dp", 1)
    product_ext = jnp.concatenate([before, product], axis=1).reshape(seqs, span, groups, group_size)
    forward_band = band(medium_filters[:, ::-1], count)
    response = jnp.einsum(
        "gtr,srgm->stgm",
        forward_band,
        product_ext.astype(jnp.float32),
        precision=lax.Precision.HIGHEST,
    ).reshape(seqs, count, channels)
    position = lax.axis_index("dp") * count + jnp.arange(count, dtype=jnp.int32)
    live = (position[None, :] < lengths[:, None])[:, :, None]
    mixed = jnp.where(live, response, 0.0).astype(jnp.bfloat16)
    upstream = jnp.where(live, cotangent, jnp.zeros_like(cotangent))
    after = shifted(upstream[:, : taps - 1], "dp", -1)
    upstream_ext = jnp.concatenate([upstream, after], axis=1).reshape(
        seqs, span, groups, group_size
    )
    backward_band = band(medium_filters, count)
    product_grad = jnp.einsum(
        "gtr,srgm->stgm",
        backward_band,
        upstream_ext.astype(jnp.float32),
        precision=lax.Precision.HIGHEST,
    ).reshape(seqs, count, channels)
    correlation = jnp.einsum(
        "stgm,srgm->gtr",
        upstream.reshape(seqs, count, groups, group_size),
        product_ext,
        preferred_element_type=jnp.float32,
    )
    medium_local = band_sums(correlation, count, taps)
    smooth_grad = jnp.stack([product_grad * smoothed[1], product_grad * smoothed[0]])
    short_local = filter_terms(smooth_grad, extended, count, short_width)
    ahead_rows = shifted(smooth_grad[:, :, : short_width - 1], "dp", -1)
    pair_grad = short_ahead(
        jnp.concatenate([smooth_grad, ahead_rows], axis=2), short_filters, count
    )
    short_grad, medium_grad = lax.psum((short_local, medium_local), "dp")
    outgoing = (
        pair_grad.astype(jnp.bfloat16).transpose(1, 2, 0, 3).reshape(seqs * count, 2 * channels)
    )
    flat_features = features.reshape(seqs * count, -1)
    grads = lax.psum_scatter(
        lax.dot_general(
            flat_features, outgoing, (((0,), (0,)), ((), ())), preferred_element_type=jnp.float32
        ).astype(jnp.bfloat16),
        "dp",
        scatter_dimension=0,
        tiled=True,
    ).astype(jnp.float32)
    key_grad = grads[:, :channels].astype(jnp.bfloat16)
    value_grad = grads[:, channels:].astype(jnp.bfloat16)
    return (mixed, key_grad, value_grad, short_grad, medium_grad)


def hyena_kernel(
    taps,
    group,
    lengths_ref,
    keys_ref,
    values_ref,
    cot_ref,
    short_ref,
    medium_ref,
    reversed_ref,
    mixed_ref,
    key_act_ref,
    value_act_ref,
    short_grad_ref,
    sums_ref,
    pad_ref,
    smooth_ref,
    grad_ref,
    product_ref,
    upstream_ref,
    ahead_band,
    behind_band,
    corr_ref,
    short_acc,
):
    blocks, seqs, count, lanes = keys_ref.shape
    halves = count // BLOCK
    steps = blocks * halves
    length = blocks * count
    groups = lanes // group
    wide = seqs * lanes

    for g in range(groups):
        rows = pl.ds(g * BLOCK, BLOCK)
        base = jnp.broadcast_to(reversed_ref[g : g + 1, :], (BLOCK, 2 * BLOCK))
        behind_band[rows, :] = pltpu.roll(base, 0, 1, stride=1, stride_axis=0).astype(jnp.bfloat16)
        base = jnp.broadcast_to(medium_ref[g : g + 1, :], (BLOCK, 2 * BLOCK))
        ahead_band[rows, :] = pltpu.roll(base, 0, 1, stride=1, stride_axis=0).astype(jnp.bfloat16)

    zeros8 = jnp.zeros((8, lanes), jnp.float32)
    zeros_block = jnp.zeros((BLOCK, lanes), jnp.bfloat16)
    for s in range(seqs):
        for branch in range(2):
            pad_ref[branch, s, pl.ds(0, 8), :] = zeros8
            grad_ref[branch, s, pl.ds(length, 8), :] = zeros8
        product_ref[pl.ds(0, BLOCK), pl.ds(s * lanes, lanes)] = zeros_block
        upstream_ref[pl.ds(length, BLOCK), pl.ds(s * lanes, lanes)] = zeros_block

    def smooth(step, carry):
        block, half = step // halves, step % halves
        source = pl.ds(pl.multiple_of(half * BLOCK, BLOCK), BLOCK)
        begin = pl.multiple_of(step * BLOCK, BLOCK)
        place = lax.broadcasted_iota(jnp.int32, (BLOCK, lanes), 0) + begin
        for s in range(seqs):
            parts = []
            for branch, ref in ((0, keys_ref), (1, values_ref)):
                now = ref[block, s, source, :].astype(jnp.float32)
                pad_ref[branch, s, pl.ds(begin + 8, BLOCK), :] = now
                window = pad_ref[branch, s, pl.ds(begin, BLOCK + 8), :]
                total = short_ref[branch, 0:1, :] * now
                for tap in range(1, taps):
                    total += short_ref[branch, tap : tap + 1, :] * window[8 - tap : 8 - tap + BLOCK]
                smooth_ref[branch, s, pl.ds(begin, BLOCK), :] = total
                parts.append(total)
            columns = pl.ds(s * lanes, lanes)
            product_ref[pl.ds(begin + BLOCK, BLOCK), columns] = (parts[0] * parts[1]).astype(
                jnp.bfloat16
            )
            cot = cot_ref[block, s, source, :].astype(jnp.float32)
            upstream_ref[pl.ds(begin, BLOCK), columns] = jnp.where(
                place < lengths_ref[s], cot, 0.0
            ).astype(jnp.bfloat16)
        return carry

    lax.fori_loop(0, steps, smooth, 0)

    lane_group = lax.broadcasted_iota(jnp.int32, (BLOCK, wide), 1) % lanes // group
    corr_ref[...] = jnp.zeros_like(corr_ref)
    short_acc[...] = jnp.zeros_like(short_acc)

    def own(stacked):
        chosen = stacked[0:BLOCK]
        for g in range(1, groups):
            chosen = jnp.where(lane_group == g, stacked[g * BLOCK : (g + 1) * BLOCK], chosen)
        return chosen

    def mix(step, carry):
        block, half = step // halves, step % halves
        source = pl.ds(pl.multiple_of(half * BLOCK, BLOCK), BLOCK)
        begin = pl.multiple_of(step * BLOCK, BLOCK)
        place = lax.broadcasted_iota(jnp.int32, (BLOCK, lanes), 0) + begin
        past = product_ref[pl.ds(begin, 2 * BLOCK), :]
        response = own(jnp.dot(behind_band[...], past, preferred_element_type=jnp.float32))
        future = upstream_ref[pl.ds(begin, 2 * BLOCK), :]
        product_grad = own(jnp.dot(ahead_band[...], future, preferred_element_type=jnp.float32))
        here = future[0:BLOCK]
        apart = jnp.concatenate(
            [jnp.where(lane_group == g, here, jnp.zeros_like(here)) for g in range(groups)], axis=0
        )
        corr_ref[...] += lax.dot_general(
            apart, past, (((1,), (1,)), ((), ())), preferred_element_type=jnp.float32
        )
        for s in range(seqs):
            columns = slice(s * lanes, (s + 1) * lanes)
            mixed_ref[block, s, source, :] = jnp.where(
                place < lengths_ref[s], response[:, columns], 0.0
            ).astype(jnp.bfloat16)
            for branch in range(2):
                grad = product_grad[:, columns] * smooth_ref[1 - branch, s, pl.ds(begin, BLOCK), :]
                grad_ref[branch, s, pl.ds(begin, BLOCK), :] = grad
                window = pad_ref[branch, s, pl.ds(begin, BLOCK + 8), :]
                for tap in range(taps):
                    term = grad * window[8 - tap : 8 - tap + BLOCK]
                    short_acc[branch, tap] += jnp.sum(term.reshape(BLOCK // 8, 8, lanes), axis=0)
        return carry

    lax.fori_loop(0, steps, mix, 0)

    def back(step, carry):
        block, half = step // halves, step % halves
        source = pl.ds(pl.multiple_of(half * BLOCK, BLOCK), BLOCK)
        begin = pl.multiple_of(step * BLOCK, BLOCK)
        for s in range(seqs):
            for branch, ref in ((0, key_act_ref), (1, value_act_ref)):
                window = grad_ref[branch, s, pl.ds(begin, BLOCK + 8), :]
                total = short_ref[branch, 0:1, :] * window[0:BLOCK]
                for tap in range(1, taps):
                    total += short_ref[branch, tap : tap + 1, :] * window[tap : tap + BLOCK]
                ref[block, s, source, :] = total.astype(jnp.bfloat16)
        return carry

    lax.fori_loop(0, steps, back, 0)

    for branch in range(2):
        for tap in range(8):
            if tap < taps:
                short_grad_ref[branch, tap : tap + 1, :] = jnp.sum(
                    short_acc[branch, tap], axis=0, keepdims=True
                )
            else:
                short_grad_ref[branch, tap : tap + 1, :] = jnp.zeros((1, lanes), jnp.float32)
    for g in range(groups):
        rows = BLOCK
        total = corr_ref[pl.ds(g * BLOCK, BLOCK), :]
        while rows > 1:
            rows //= 2
            total = total[:rows] + pltpu.roll(total[rows:], 2 * BLOCK - rows, 1)
        sums_ref[g : g + 1, :] = total


def hyena(keys, values, cotangent, short_filters, medium_filters, lengths):
    blocks, seqs, count, lanes = keys.shape
    groups, medium = medium_filters.shape
    taps = short_filters.shape[-1]
    length = blocks * count
    short = jnp.pad(short_filters.transpose(0, 2, 1), ((0, 0), (0, 8 - taps), (0, 0)))
    forward = jnp.pad(medium_filters, ((0, 0), (0, 2 * BLOCK - medium)))
    backward = jnp.pad(
        medium_filters[:, ::-1], ((0, 0), (BLOCK + 1 - medium, BLOCK - 1))
    )
    vmem = pl.BlockSpec(memory_space=pltpu.VMEM)
    acts = jax.ShapeDtypeStruct(keys.shape, jnp.bfloat16)
    mixed, key_act, value_act, short_grad, sums = pl.pallas_call(
        functools.partial(hyena_kernel, taps, lanes // groups),
        out_shape=(
            acts,
            acts,
            acts,
            jax.ShapeDtypeStruct((2, 8, lanes), jnp.float32),
            jax.ShapeDtypeStruct((groups, 2 * BLOCK), jnp.float32),
        ),
        in_specs=[pl.BlockSpec(memory_space=pltpu.SMEM)] + [vmem] * 6,
        out_specs=[vmem] * 5,
        scratch_shapes=[
            pltpu.VMEM((2, seqs, length + 8, lanes), jnp.float32),
            pltpu.VMEM((2, seqs, length, lanes), jnp.float32),
            pltpu.VMEM((2, seqs, length + 8, lanes), jnp.float32),
            pltpu.VMEM((length + BLOCK, seqs * lanes), jnp.bfloat16),
            pltpu.VMEM((length + BLOCK, seqs * lanes), jnp.bfloat16),
            pltpu.VMEM((groups * BLOCK, 2 * BLOCK), jnp.bfloat16),
            pltpu.VMEM((groups * BLOCK, 2 * BLOCK), jnp.bfloat16),
            pltpu.VMEM((groups * BLOCK, 2 * BLOCK), jnp.float32),
            pltpu.VMEM((2, taps, 8, lanes), jnp.float32),
        ],
        compiler_params=pltpu.CompilerParams(vmem_limit_bytes=40 * 1024 * 1024),
        cost_estimate=pl.CostEstimate(
            flops=12 * groups * length * seqs * 2 * BLOCK * lanes,
            bytes_accessed=12 * length * seqs * lanes,
            transcendentals=0,
        ),
    )(lengths, keys, values, cotangent, short, forward, backward)
    medium_grad = sums[:, BLOCK - medium + 1 : BLOCK + 1][:, ::-1]
    return mixed, key_act, value_act, short_grad[:, :taps].transpose(0, 2, 1), medium_grad


def by_channels(inputs, key_panel, value_panel, short_filters, medium_filters, lengths, cotangent):
    seqs, count, width = inputs.shape
    blocks = lax.axis_size("dp")
    shard = lax.axis_size("shard")
    channels = key_panel.shape[1]
    lanes = channels // blocks
    groups = medium_filters.shape[0] // blocks
    mine = lax.axis_index("dp")
    cores = shard // blocks
    across = [[b * cores + core for b in range(blocks)] for core in range(cores)]
    paired = [[b * cores + core for core in range(cores)] for b in range(blocks)]
    spread = lax.all_gather(inputs, "shard", axis_index_groups=across)
    turned = lax.all_to_all(spread, "dp", split_axis=0, concat_axis=0, tiled=True)
    features = lax.all_gather(turned, "shard", axis_index_groups=paired)
    features = features.reshape(cores, blocks * seqs * count, width)
    cot = lax.all_to_all(
        cotangent.reshape(seqs, count, blocks, lanes), "dp", split_axis=2, concat_axis=0
    )

    def project(panel):
        partial = jnp.einsum(
            "cnf,cfm->nm",
            features,
            panel.reshape(cores, width, channels),
            preferred_element_type=jnp.float32,
        ).astype(jnp.bfloat16)
        owned = lax.psum_scatter(partial, "dp", scatter_dimension=1, tiled=True)
        return owned.reshape(blocks, seqs, count, lanes)

    keys, values = project(key_panel), project(value_panel)
    short = lax.dynamic_slice_in_dim(short_filters, mine * lanes, lanes, 1)
    medium = lax.dynamic_slice_in_dim(medium_filters, mine * groups, groups, 0)
    mixed, key_act, value_act, short_grad, medium_grad = hyena(
        keys, values, cot, short, medium, lengths
    )

    def panel_grad(act):
        gathered = lax.all_gather(act.reshape(-1, lanes), "dp", axis=1, tiled=True)
        return (
            jnp.einsum("cnf,nm->cfm", features, gathered, preferred_element_type=jnp.float32)
            .astype(jnp.bfloat16)
            .reshape(cores * width, channels)
        )

    key_grad, value_grad = panel_grad(key_act), panel_grad(value_act)
    mixed = lax.all_to_all(mixed, "dp", split_axis=0, concat_axis=2, tiled=False)
    mixed = mixed.reshape(seqs, count, channels)
    short_grad = lax.all_gather(short_grad, "dp", axis=1, tiled=True)
    medium_grad = lax.all_gather(medium_grad, "dp", axis=0, tiled=True)
    return (mixed, key_grad, value_grad, short_grad, medium_grad)


def shards(inputs, key_panel, value_panel, short_filters, medium_filters, lengths, cotangent):
    blocks, shard = lax.axis_size("dp"), lax.axis_size("shard")
    channels = key_panel.shape[1]
    whole_lanes = channels % (blocks * BLOCK) == 0
    whole_rows = shard % blocks == 0 and inputs.shape[1] % BLOCK == 0
    plan = by_channels if whole_lanes and whole_rows else by_positions
    return plan(
        inputs, key_panel, value_panel, short_filters, medium_filters, lengths, cotangent
    )


def solution(mesh):
    return jax.shard_map(
        shards,
        mesh=mesh,
        in_specs=(
            P(None, "dp", "shard"),
            P("dp", "shard"),
            P("dp", "shard"),
            P(None, "shard", None),
            P("shard", None),
            P(),
            P(None, "dp", "shard"),
        ),
        out_specs=(
            P(None, "dp", "shard"),
            P("dp", "shard"),
            P("dp", "shard"),
            P(None, "shard", None),
            P("shard", None),
        ),
        check_vma=False,
    )
```

```python
import functools

import jax
import jax.numpy as jnp
from jax import lax
from jax.experimental import pallas as pl
from jax.experimental.pallas import tpu as pltpu
from jax.sharding import PartitionSpec as P

BLOCK = 128


def shifted(value, axis, steps):
    count = lax.axis_size(axis)
    first, last = (max(0, -steps), min(count, count - steps))
    return lax.ppermute(value, axis, [(source, source + steps) for source in range(first, last)])


def band(filters, count):
    groups, taps = filters.shape
    width = count + taps - 1
    padded = jnp.concatenate([filters, jnp.zeros((groups, count), jnp.float32)], axis=1)
    tiled = jnp.tile(padded, (1, count))[:, : count * width]
    return tiled.reshape(groups, count, width)


def band_sums(correlation, count, taps):
    groups, _, width = correlation.shape
    flat = correlation.reshape(groups, count * width)
    padded = jnp.concatenate([flat, jnp.zeros((groups, count), jnp.float32)], axis=1)
    skewed = padded.reshape(groups, count, width + 1)
    return jnp.sum(skewed, axis=1)[:, :taps][:, ::-1]


def short_taps(extended, filters, count):
    width = filters.shape[-1]
    total = jnp.zeros(extended.shape[:2] + (count, extended.shape[3]), jnp.float32)
    for tap in range(width):
        begin = width - 1 - tap
        total = total + filters[:, None, None, :, tap] * extended[
            :, :, begin : begin + count
        ].astype(jnp.float32)
    return total


def short_ahead(extended, filters, count):
    width = filters.shape[-1]
    total = jnp.zeros(extended.shape[:2] + (count, extended.shape[3]), jnp.float32)
    for tap in range(width):
        total = total + filters[:, None, None, :, tap] * extended[:, :, tap : tap + count]
    return total


def filter_terms(grads, extended, count, width):
    columns = []
    for tap in range(width):
        begin = width - 1 - tap
        columns.append(
            jnp.sum(grads * extended[:, :, begin : begin + count].astype(jnp.float32), axis=(1, 2))
        )
    return jnp.stack(columns, axis=-1)


def by_positions(inputs, key_panel, value_panel, short_filters, medium_filters, lengths, cotangent):
    seqs, count, local_width = inputs.shape
    channels = key_panel.shape[1]
    groups, taps = medium_filters.shape
    group_size = channels // groups
    short_width = short_filters.shape[-1]
    span = count + taps - 1
    gathered = (
        lax.all_gather(key_panel, "dp", axis=0, tiled=True),
        lax.all_gather(value_panel, "dp", axis=0, tiled=True),
    )
    panels = jnp.concatenate([gathered[0], gathered[1]], axis=1)
    features = lax.all_gather(inputs, "shard", axis=2, tiled=True)
    projected = jnp.dot(
        features.reshape(seqs * count, -1), panels, preferred_element_type=jnp.float32
    )
    paired = projected.astype(jnp.bfloat16).reshape(seqs, count, 2, channels).transpose(2, 0, 1, 3)
    head_rows = shifted(paired[:, :, count - (short_width - 1) :], "dp", 1)
    extended = jnp.concatenate([head_rows, paired], axis=2)
    smoothed = short_taps(extended, short_filters, count)
    product = (smoothed[0] * smoothed[1]).astype(jnp.bfloat16)
    before = shifted(product[:, count - (taps - 1) :], "dp", 1)
    product_ext = jnp.concatenate([before, product], axis=1).reshape(seqs, span, groups, group_size)
    forward_band = band(medium_filters[:, ::-1], count)
    response = jnp.einsum(
        "gtr,srgm->stgm",
        forward_band,
        product_ext.astype(jnp.float32),
        precision=lax.Precision.HIGHEST,
    ).reshape(seqs, count, channels)
    position = lax.axis_index("dp") * count + jnp.arange(count, dtype=jnp.int32)
    live = (position[None, :] < lengths[:, None])[:, :, None]
    mixed = jnp.where(live, response, 0.0).astype(jnp.bfloat16)
    upstream = jnp.where(live, cotangent, jnp.zeros_like(cotangent))
    after = shifted(upstream[:, : taps - 1], "dp", -1)
    upstream_ext = jnp.concatenate([upstream, after], axis=1).reshape(
        seqs, span, groups, group_size
    )
    backward_band = band(medium_filters, count)
    product_grad = jnp.einsum(
        "gtr,srgm->stgm",
        backward_band,
        upstream_ext.astype(jnp.float32),
        precision=lax.Precision.HIGHEST,
    ).reshape(seqs, count, channels)
    correlation = jnp.einsum(
        "stgm,srgm->gtr",
        upstream.reshape(seqs, count, groups, group_size),
        product_ext,
        preferred_element_type=jnp.float32,
    )
    medium_local = band_sums(correlation, count, taps)
    smooth_grad = jnp.stack([product_grad * smoothed[1], product_grad * smoothed[0]])
    short_local = filter_terms(smooth_grad, extended, count, short_width)
    ahead_rows = shifted(smooth_grad[:, :, : short_width - 1], "dp", -1)
    pair_grad = short_ahead(
        jnp.concatenate([smooth_grad, ahead_rows], axis=2), short_filters, count
    )
    short_grad, medium_grad = lax.psum((short_local, medium_local), "dp")
    outgoing = (
        pair_grad.astype(jnp.bfloat16).transpose(1, 2, 0, 3).reshape(seqs * count, 2 * channels)
    )
    flat_features = features.reshape(seqs * count, -1)
    grads = lax.psum_scatter(
        lax.dot_general(
            flat_features, outgoing, (((0,), (0,)), ((), ())), preferred_element_type=jnp.float32
        ).astype(jnp.bfloat16),
        "dp",
        scatter_dimension=0,
        tiled=True,
    ).astype(jnp.float32)
    key_grad = grads[:, :channels].astype(jnp.bfloat16)
    value_grad = grads[:, channels:].astype(jnp.bfloat16)
    return (mixed, key_grad, value_grad, short_grad, medium_grad)


def hyena_kernel(
    taps,
    group,
    lengths_ref,
    keys_ref,
    values_ref,
    cot_ref,
    short_ref,
    medium_ref,
    reversed_ref,
    mixed_ref,
    key_act_ref,
    value_act_ref,
    short_grad_ref,
    sums_ref,
    pad_ref,
    smooth_ref,
    grad_ref,
    product_ref,
    upstream_ref,
    ahead_band,
    behind_band,
    corr_ref,
    short_acc,
):
    seqs, blocks, count, lanes = keys_ref.shape
    halves = count // BLOCK
    steps = blocks * halves
    length = blocks * count
    groups = lanes // group
    wide = seqs * lanes

    for g in range(groups):
        rows = pl.ds(g * BLOCK, BLOCK)
        base = jnp.broadcast_to(reversed_ref[g : g + 1, :], (BLOCK, 2 * BLOCK))
        behind_band[rows, :] = pltpu.roll(base, 0, 1, stride=1, stride_axis=0).astype(jnp.bfloat16)
        base = jnp.broadcast_to(medium_ref[g : g + 1, :], (BLOCK, 2 * BLOCK))
        ahead_band[rows, :] = pltpu.roll(base, 0, 1, stride=1, stride_axis=0).astype(jnp.bfloat16)

    zeros8 = jnp.zeros((8, lanes), jnp.float32)
    zeros_block = jnp.zeros((BLOCK, lanes), jnp.bfloat16)
    for s in range(seqs):
        for branch in range(2):
            pad_ref[branch, s, pl.ds(0, 8), :] = zeros8
            grad_ref[branch, s, pl.ds(length, 8), :] = zeros8
        product_ref[pl.ds(0, BLOCK), pl.ds(s * lanes, lanes)] = zeros_block
        upstream_ref[pl.ds(length, BLOCK), pl.ds(s * lanes, lanes)] = zeros_block

    def smooth(step, carry):
        block, half = step // halves, step % halves
        source = pl.ds(pl.multiple_of(half * BLOCK, BLOCK), BLOCK)
        begin = pl.multiple_of(step * BLOCK, BLOCK)
        place = lax.broadcasted_iota(jnp.int32, (BLOCK, lanes), 0) + begin
        for s in range(seqs):
            parts = []
            for branch, ref in ((0, keys_ref), (1, values_ref)):
                now = ref[s, block, source, :].astype(jnp.float32)
                pad_ref[branch, s, pl.ds(begin + 8, BLOCK), :] = now
                window = pad_ref[branch, s, pl.ds(begin, BLOCK + 8), :]
                total = short_ref[branch, 0:1, :] * now
                for tap in range(1, taps):
                    total += short_ref[branch, tap : tap + 1, :] * window[8 - tap : 8 - tap + BLOCK]
                smooth_ref[branch, s, pl.ds(begin, BLOCK), :] = total
                parts.append(total)
            columns = pl.ds(s * lanes, lanes)
            product_ref[pl.ds(begin + BLOCK, BLOCK), columns] = (parts[0] * parts[1]).astype(
                jnp.bfloat16
            )
            cot = cot_ref[block, s, source, :].astype(jnp.float32)
            upstream_ref[pl.ds(begin, BLOCK), columns] = jnp.where(
                place < lengths_ref[s], cot, 0.0
            ).astype(jnp.bfloat16)
        return carry

    lax.fori_loop(0, steps, smooth, 0)

    lane_group = lax.broadcasted_iota(jnp.int32, (BLOCK, wide), 1) % lanes // group
    corr_ref[...] = jnp.zeros_like(corr_ref)
    short_acc[...] = jnp.zeros_like(short_acc)

    def own(stacked):
        chosen = stacked[0:BLOCK]
        for g in range(1, groups):
            chosen = jnp.where(lane_group == g, stacked[g * BLOCK : (g + 1) * BLOCK], chosen)
        return chosen

    def mix(step, carry):
        block, half = step // halves, step % halves
        source = pl.ds(pl.multiple_of(half * BLOCK, BLOCK), BLOCK)
        begin = pl.multiple_of(step * BLOCK, BLOCK)
        place = lax.broadcasted_iota(jnp.int32, (BLOCK, lanes), 0) + begin
        past = product_ref[pl.ds(begin, 2 * BLOCK), :]
        response = own(jnp.dot(behind_band[...], past, preferred_element_type=jnp.float32))
        future = upstream_ref[pl.ds(begin, 2 * BLOCK), :]
        product_grad = own(jnp.dot(ahead_band[...], future, preferred_element_type=jnp.float32))
        here = future[0:BLOCK]
        apart = jnp.concatenate(
            [jnp.where(lane_group == g, here, jnp.zeros_like(here)) for g in range(groups)], axis=0
        )
        corr_ref[...] += lax.dot_general(
            apart, past, (((1,), (1,)), ((), ())), preferred_element_type=jnp.float32
        )
        for s in range(seqs):
            columns = slice(s * lanes, (s + 1) * lanes)
            mixed_ref[block, s, source, :] = jnp.where(
                place < lengths_ref[s], response[:, columns], 0.0
            ).astype(jnp.bfloat16)
            for branch in range(2):
                grad = product_grad[:, columns] * smooth_ref[1 - branch, s, pl.ds(begin, BLOCK), :]
                grad_ref[branch, s, pl.ds(begin, BLOCK), :] = grad
                window = pad_ref[branch, s, pl.ds(begin, BLOCK + 8), :]
                for tap in range(taps):
                    term = grad * window[8 - tap : 8 - tap + BLOCK]
                    short_acc[branch, tap] += jnp.sum(term.reshape(BLOCK // 8, 8, lanes), axis=0)
        return carry

    lax.fori_loop(0, steps, mix, 0)

    def back(step, carry):
        block, half = step // halves, step % halves
        source = pl.ds(pl.multiple_of(half * BLOCK, BLOCK), BLOCK)
        begin = pl.multiple_of(step * BLOCK, BLOCK)
        for s in range(seqs):
            for branch, ref in ((0, key_act_ref), (1, value_act_ref)):
                window = grad_ref[branch, s, pl.ds(begin, BLOCK + 8), :]
                total = short_ref[branch, 0:1, :] * window[0:BLOCK]
                for tap in range(1, taps):
                    total += short_ref[branch, tap : tap + 1, :] * window[tap : tap + BLOCK]
                ref[s, block, source, :] = total.astype(jnp.bfloat16)
        return carry

    lax.fori_loop(0, steps, back, 0)

    for branch in range(2):
        for tap in range(8):
            if tap < taps:
                short_grad_ref[branch, tap : tap + 1, :] = jnp.sum(
                    short_acc[branch, tap], axis=0, keepdims=True
                )
            else:
                short_grad_ref[branch, tap : tap + 1, :] = jnp.zeros((1, lanes), jnp.float32)
    for g in range(groups):
        rows = BLOCK
        total = corr_ref[pl.ds(g * BLOCK, BLOCK), :]
        while rows > 1:
            rows //= 2
            total = total[:rows] + pltpu.roll(total[rows:], 2 * BLOCK - rows, 1)
        sums_ref[g : g + 1, :] = total


def hyena(keys, values, cotangent, short_filters, medium_filters, lengths):
    seqs, blocks, count, lanes = keys.shape
    groups, medium = medium_filters.shape
    taps = short_filters.shape[-1]
    length = blocks * count
    short = jnp.pad(short_filters.transpose(0, 2, 1), ((0, 0), (0, 8 - taps), (0, 0)))
    forward = jnp.pad(medium_filters, ((0, 0), (0, 2 * BLOCK - medium)))
    backward = jnp.pad(
        medium_filters[:, ::-1], ((0, 0), (BLOCK + 1 - medium, BLOCK - 1))
    )
    vmem = pl.BlockSpec(memory_space=pltpu.VMEM)
    acts = jax.ShapeDtypeStruct(keys.shape, jnp.bfloat16)
    mixed, key_act, value_act, short_grad, sums = pl.pallas_call(
        functools.partial(hyena_kernel, taps, lanes // groups),
        out_shape=(
            jax.ShapeDtypeStruct(cotangent.shape, jnp.bfloat16),
            acts,
            acts,
            jax.ShapeDtypeStruct((2, 8, lanes), jnp.float32),
            jax.ShapeDtypeStruct((groups, 2 * BLOCK), jnp.float32),
        ),
        in_specs=[pl.BlockSpec(memory_space=pltpu.SMEM)] + [vmem] * 6,
        out_specs=[vmem] * 5,
        scratch_shapes=[
            pltpu.VMEM((2, seqs, length + 8, lanes), jnp.float32),
            pltpu.VMEM((2, seqs, length, lanes), jnp.float32),
            pltpu.VMEM((2, seqs, length + 8, lanes), jnp.float32),
            pltpu.VMEM((length + BLOCK, seqs * lanes), jnp.bfloat16),
            pltpu.VMEM((length + BLOCK, seqs * lanes), jnp.bfloat16),
            pltpu.VMEM((groups * BLOCK, 2 * BLOCK), jnp.bfloat16),
            pltpu.VMEM((groups * BLOCK, 2 * BLOCK), jnp.bfloat16),
            pltpu.VMEM((groups * BLOCK, 2 * BLOCK), jnp.float32),
            pltpu.VMEM((2, taps, 8, lanes), jnp.float32),
        ],
        compiler_params=pltpu.CompilerParams(vmem_limit_bytes=40 * 1024 * 1024),
        cost_estimate=pl.CostEstimate(
            flops=12 * groups * length * seqs * 2 * BLOCK * lanes,
            bytes_accessed=12 * length * seqs * lanes,
            transcendentals=0,
        ),
    )(lengths, keys, values, cotangent, short, forward, backward)
    medium_grad = sums[:, BLOCK - medium + 1 : BLOCK + 1][:, ::-1]
    return mixed, key_act, value_act, short_grad[:, :taps].transpose(0, 2, 1), medium_grad


def remote(source, target, send, recv, dp, shard):
    return pltpu.make_async_remote_copy(
        src_ref=source,
        dst_ref=target,
        send_sem=send,
        recv_sem=recv,
        device_id={"dp": dp, "shard": shard},
        device_id_type=pl.DeviceIdType.MESH,
    )


def front_kernel(
    x_ref,
    key_ref,
    value_ref,
    cot_ref,
    keys_ref,
    values_ref,
    cot_out,
    features_out,
    line,
    features,
    panels,
    own,
    outgoing,
    incoming,
    cot_in,
    line_send,
    line_recv,
    plane_send,
    plane_recv,
    core_send,
    core_recv,
    sum_send,
    sum_recv,
    cot_send,
    cot_recv,
    local,
    saved,
):
    seqs, count, width = x_ref.shape
    blocks, lanes = cot_in.shape[0], cot_in.shape[-1]
    rows = count // 2
    p, shard = lax.axis_index("dp"), lax.axis_index("shard")
    z, core = shard // 2, shard % 2
    sibling = z * 2 + (1 - core)
    peers = [(p + j) % blocks for j in range(blocks)]
    froms = [(p + blocks - j) % blocks for j in range(blocks)]

    barrier = pltpu.get_barrier_semaphore()

    def greet(dp, to):
        pl.semaphore_signal(
            barrier,
            inc=1,
            device_id={"dp": dp, "shard": to},
            device_id_type=pl.DeviceIdType.MESH,
        )

    greet(p, sibling)
    for j in range(1, blocks):
        greet(peers[j], shard)

    for step in (2, 2 * blocks - 2):
        greet(p, (shard + step) % (2 * blocks))
    pl.semaphore_wait(barrier, blocks + 2)

    def part(half):
        return pl.ds(half * rows, rows)

    def held(h, layer, w, half):
        return x_ref.at[w, part(half)] if h == 0 else line.at[layer, w, part(half)]

    def line_copy(h, layer, w, half, way):
        piece = w * 2 + half
        return remote(
            held(h, layer, w, half),
            line.at[layer, w, part(half)],
            line_send.at[way, layer, piece],
            line_recv.at[layer, piece],
            p,
            shard + 2 * (1 - 2 * way),
        )

    def plane_copy(h, layer, w, half):
        piece = w * 2 + half
        return remote(
            held(h, layer, w, half),
            features.at[core, w, p, part(half)],
            plane_send.at[layer, piece],
            plane_recv.at[p, piece],
            layer,
            shard,
        )

    def plane_arrival(block, w, half):
        piece = w * 2 + half
        place = features.at[core, w, block, part(half)]
        return remote(
            place, place, plane_send.at[block, piece], plane_recv.at[block, piece], block, shard
        )

    def core_copy(source, block, w, half):
        piece = w * 2 + half
        return remote(
            source,
            features.at[core, w, block, part(half)],
            core_send.at[block, piece],
            core_recv.at[block, piece],
            p,
            sibling,
        )

    def core_arrival(block, w, half):
        piece = w * 2 + half
        place = features.at[1 - core, w, block, part(half)]
        return remote(
            place, place, core_send.at[block, piece], core_recv.at[block, piece], p, sibling
        )

    def keep_copy(h, layer, w, half):
        return pltpu.make_async_copy(
            held(h, layer, w, half), features.at[core, w, p, part(half)], local.at[w * 2 + half]
        )

    def steps(h):
        if h == 0:
            return [(0, z, None, z < blocks - 1), (1, z, None, z > 0)]
        return [
            (0, z - h, z - h >= 0, z < blocks - 1),
            (1, z + h, z + h < blocks, z > 0),
        ]

    def dispatch(h, layer, w, half):
        @pl.when(layer == p)
        def _():
            keep_copy(h, layer, w, half).start()
            core_copy(held(h, layer, w, half), p, w, half).start()

        @pl.when(layer != p)
        def _():
            plane_copy(h, layer, w, half).start()

    def hop(w, h):
        for half in range(2):
            if h == 0:
                for way, layer, _, onward in steps(0):

                    @pl.when(onward)
                    def _():
                        line_copy(0, layer, w, half, way).start()

                dispatch(0, z, w, half)
            else:
                for way, layer, valid, onward in steps(h):

                    @pl.when(valid)
                    def _():
                        line_copy(h, layer, w, half, way).wait_recv()

                        @pl.when(onward)
                        def _():
                            line_copy(h, layer, w, half, way).start()

                        dispatch(h, layer, w, half)

    def share(w):
        for half in range(2):
            for j in range(1, blocks):
                plane_arrival(froms[j], w, half).wait_recv()
                place = features.at[core, w, froms[j], part(half)]
                core_copy(place, froms[j], w, half).start()

    def save_copy(w):
        return pltpu.make_async_copy(features.at[:, w], features_out.at[:, w], saved.at[w])

    def complete(w):
        for half in range(2):
            for j in range(blocks):
                core_arrival(froms[j], w, half).wait_recv()
            keep_copy(0, z, w, half).wait()
        save_copy(w).start()

    def sum_copy(w, j):
        return remote(
            outgoing.at[w, j - 1],
            incoming.at[w, j - 1],
            sum_send.at[w, j - 1],
            sum_recv.at[w, j - 1],
            peers[j],
            shard,
        )

    def project(w, j):
        def tile(i, carry):
            total = jnp.zeros((count, 2 * lanes), jnp.float32)
            for c in range(2):
                total += jnp.dot(
                    features[c, w, i], panels[peers[j], c], preferred_element_type=jnp.float32
                )
            if j == 0:
                own[w, i] = total
            else:
                outgoing[w, j - 1, i] = total.astype(jnp.bfloat16)
            return carry

        lax.fori_loop(0, blocks, tile, 0)
        if j > 0:
            sum_copy(w, j).start()

    def cot_copy(j):
        place = pl.ds(pl.multiple_of(peers[j] * lanes, lanes), lanes)
        return remote(
            cot_ref.at[:, :, place],
            cot_in.at[p],
            cot_send.at[j],
            cot_recv.at[p],
            peers[j],
            shard,
        )

    def cot_arrival(j):
        return remote(
            cot_in.at[froms[j]],
            cot_in.at[froms[j]],
            cot_send.at[j],
            cot_recv.at[froms[j]],
            froms[j],
            shard,
        )

    hop(0, 0)
    for r in range(blocks):
        for c in range(2):
            source = pl.ds(c * width, width)
            columns = slice(r * lanes, (r + 1) * lanes)
            panels[r, c, :, 0:lanes] = key_ref[source, columns]
            panels[r, c, :, lanes : 2 * lanes] = value_ref[source, columns]
    for h in range(1, blocks):
        hop(0, h)
    hop(1, 0)
    share(0)
    hop(1, 1)
    complete(0)
    project(0, 2)
    project(0, 1)
    hop(1, 2)
    project(0, 3)
    hop(1, 3)
    project(0, 0)
    share(1)
    for j in range(1, blocks):
        cot_copy(j).start()
    cot_in[p] = cot_ref[:, :, pl.ds(pl.multiple_of(p * lanes, lanes), lanes)]
    complete(1)
    for j in (1, 3, 2, 0):
        project(1, j)
    for j in range(1, blocks):
        cot_arrival(j).wait_recv()
    cot_out[...] = cot_in[...]
    for w in range(seqs):
        for j in range(1, blocks):
            sum_copy(w, j).wait_recv()

        def add(i, carry):
            total = own[w, i]
            for j in range(1, blocks):
                total += incoming[w, j - 1, i].astype(jnp.float32)
            keys_ref[w, i] = total[:, 0:lanes].astype(jnp.bfloat16)
            values_ref[w, i] = total[:, lanes : 2 * lanes].astype(jnp.bfloat16)
            return carry

        lax.fori_loop(0, blocks, add, 0)

    for w in range(seqs):
        save_copy(w).wait()
        for j in range(1, blocks):
            sum_copy(w, j).wait_send()
        for half in range(2):
            for j in range(blocks):
                core_copy(features.at[core, w, froms[j], part(half)], froms[j], w, half).wait_send()
            for h in range(blocks):
                for way, layer, valid, onward in steps(h):
                    if h > 0:
                        onward = jnp.logical_and(valid, onward)

                    @pl.when(onward)
                    def _():
                        line_copy(h, layer, w, half, way).wait_send()

                    if h > 0 or way == 0:
                        sent = layer != p
                        if h > 0:
                            sent = jnp.logical_and(valid, sent)

                        @pl.when(sent)
                        def _():
                            plane_copy(h, layer, w, half).wait_send()

    for j in range(1, blocks):
        cot_copy(j).wait_send()


def front(inputs, key_panel, value_panel, cotangent, blocks):
    seqs, count, width = inputs.shape
    channels = key_panel.shape[1]
    lanes = channels // blocks
    pieces = 2 * seqs
    vmem = pl.BlockSpec(memory_space=pltpu.VMEM)
    hbm = pl.BlockSpec(memory_space=pl.ANY)
    acts = jax.ShapeDtypeStruct((seqs, blocks, count, lanes), jnp.bfloat16)
    feature_shape = (2, seqs, blocks, count, width)
    dma = pltpu.SemaphoreType.DMA
    return pl.pallas_call(
        front_kernel,
        out_shape=(
            acts,
            acts,
            jax.ShapeDtypeStruct((blocks, seqs, count, lanes), jnp.bfloat16),
            jax.ShapeDtypeStruct(feature_shape, jnp.bfloat16),
        ),
        in_specs=[hbm, vmem, vmem, vmem],
        out_specs=[vmem, vmem, vmem, hbm],
        scratch_shapes=[
            pltpu.VMEM((blocks, seqs, count, width), jnp.bfloat16),
            pltpu.VMEM(feature_shape, jnp.bfloat16),
            pltpu.VMEM((blocks, 2, width, 2 * lanes), jnp.bfloat16),
            pltpu.VMEM((seqs, blocks, count, 2 * lanes), jnp.float32),
            pltpu.VMEM((seqs, blocks - 1, blocks, count, 2 * lanes), jnp.bfloat16),
            pltpu.VMEM((seqs, blocks - 1, blocks, count, 2 * lanes), jnp.bfloat16),
            pltpu.VMEM((blocks, seqs, count, lanes), jnp.bfloat16),
            dma((2, blocks, pieces)),
            dma((blocks, pieces)),
            dma((blocks, pieces)),
            dma((blocks, pieces)),
            dma((blocks, pieces)),
            dma((blocks, pieces)),
            dma((seqs, blocks - 1)),
            dma((seqs, blocks - 1)),
            dma((blocks,)),
            dma((blocks,)),
            dma((pieces,)),
            dma((seqs,)),
        ],
        compiler_params=pltpu.CompilerParams(
            collective_id=0, has_side_effects=True, vmem_limit_bytes=48 * 1024 * 1024
        ),
        cost_estimate=pl.CostEstimate(
            flops=4 * blocks * seqs * count * 2 * width * channels,
            bytes_accessed=8 * blocks * seqs * count * width,
            transcendentals=0,
        ),
    )(inputs, key_panel, value_panel, cotangent)


def by_channels(inputs, key_panel, value_panel, short_filters, medium_filters, lengths, cotangent):
    seqs, count, width = inputs.shape
    blocks = lax.axis_size("dp")
    channels = key_panel.shape[1]
    lanes = channels // blocks
    groups = medium_filters.shape[0] // blocks
    mine = lax.axis_index("dp")
    keys, values, cot, features = front(inputs, key_panel, value_panel, cotangent, blocks)
    features = features.reshape(2, blocks * seqs * count, width)
    short = lax.dynamic_slice_in_dim(short_filters, mine * lanes, lanes, 1)
    medium = lax.dynamic_slice_in_dim(medium_filters, mine * groups, groups, 0)
    mixed, key_act, value_act, short_grad, medium_grad = hyena(
        keys, values, cot, short, medium, lengths
    )

    def panel_grad(act):
        gathered = lax.all_gather(act.reshape(-1, lanes), "dp", axis=1, tiled=True)
        return (
            jnp.einsum("cnf,nm->cfm", features, gathered, preferred_element_type=jnp.float32)
            .astype(jnp.bfloat16)
            .reshape(2 * width, channels)
        )

    key_grad, value_grad = panel_grad(key_act), panel_grad(value_act)
    mixed = lax.all_to_all(mixed, "dp", split_axis=0, concat_axis=2, tiled=False)
    mixed = mixed.reshape(seqs, count, channels)
    short_grad = lax.all_gather(short_grad, "dp", axis=1, tiled=True)
    medium_grad = lax.all_gather(medium_grad, "dp", axis=0, tiled=True)
    return (mixed, key_grad, value_grad, short_grad, medium_grad)


def shards(inputs, key_panel, value_panel, short_filters, medium_filters, lengths, cotangent):
    blocks, shard = lax.axis_size("dp"), lax.axis_size("shard")
    channels = key_panel.shape[1]
    whole = channels == blocks * BLOCK and inputs.shape[1] % (2 * BLOCK) == 0
    plan = by_channels if whole and blocks == 4 and shard == 2 * blocks else by_positions
    return plan(
        inputs, key_panel, value_panel, short_filters, medium_filters, lengths, cotangent
    )


def solution(mesh):
    return jax.shard_map(
        shards,
        mesh=mesh,
        in_specs=(
            P(None, "dp", "shard"),
            P("dp", "shard"),
            P("dp", "shard"),
            P(None, "shard", None),
            P("shard", None),
            P(),
            P(None, "dp", "shard"),
        ),
        out_specs=(
            P(None, "dp", "shard"),
            P("dp", "shard"),
            P("dp", "shard"),
            P(None, "shard", None),
            P("shard", None),
        ),
        check_vma=False,
    )
```

```python
import functools

import jax
import jax.numpy as jnp
from jax import lax
from jax.experimental import pallas as pl
from jax.experimental.pallas import tpu as pltpu
from jax.sharding import PartitionSpec as P

BLOCK = 128


def shifted(value, axis, steps):
    count = lax.axis_size(axis)
    first, last = (max(0, -steps), min(count, count - steps))
    return lax.ppermute(value, axis, [(source, source + steps) for source in range(first, last)])


def band(filters, count):
    groups, taps = filters.shape
    width = count + taps - 1
    padded = jnp.concatenate([filters, jnp.zeros((groups, count), jnp.float32)], axis=1)
    tiled = jnp.tile(padded, (1, count))[:, : count * width]
    return tiled.reshape(groups, count, width)


def band_sums(correlation, count, taps):
    groups, _, width = correlation.shape
    flat = correlation.reshape(groups, count * width)
    padded = jnp.concatenate([flat, jnp.zeros((groups, count), jnp.float32)], axis=1)
    skewed = padded.reshape(groups, count, width + 1)
    return jnp.sum(skewed, axis=1)[:, :taps][:, ::-1]


def short_taps(extended, filters, count):
    width = filters.shape[-1]
    total = jnp.zeros(extended.shape[:2] + (count, extended.shape[3]), jnp.float32)
    for tap in range(width):
        begin = width - 1 - tap
        total = total + filters[:, None, None, :, tap] * extended[
            :, :, begin : begin + count
        ].astype(jnp.float32)
    return total


def short_ahead(extended, filters, count):
    width = filters.shape[-1]
    total = jnp.zeros(extended.shape[:2] + (count, extended.shape[3]), jnp.float32)
    for tap in range(width):
        total = total + filters[:, None, None, :, tap] * extended[:, :, tap : tap + count]
    return total


def filter_terms(grads, extended, count, width):
    columns = []
    for tap in range(width):
        begin = width - 1 - tap
        columns.append(
            jnp.sum(grads * extended[:, :, begin : begin + count].astype(jnp.float32), axis=(1, 2))
        )
    return jnp.stack(columns, axis=-1)


def by_positions(inputs, key_panel, value_panel, short_filters, medium_filters, lengths, cotangent):
    seqs, count, local_width = inputs.shape
    channels = key_panel.shape[1]
    groups, taps = medium_filters.shape
    group_size = channels // groups
    short_width = short_filters.shape[-1]
    span = count + taps - 1
    gathered = (
        lax.all_gather(key_panel, "dp", axis=0, tiled=True),
        lax.all_gather(value_panel, "dp", axis=0, tiled=True),
    )
    panels = jnp.concatenate([gathered[0], gathered[1]], axis=1)
    features = lax.all_gather(inputs, "shard", axis=2, tiled=True)
    projected = jnp.dot(
        features.reshape(seqs * count, -1), panels, preferred_element_type=jnp.float32
    )
    paired = projected.astype(jnp.bfloat16).reshape(seqs, count, 2, channels).transpose(2, 0, 1, 3)
    head_rows = shifted(paired[:, :, count - (short_width - 1) :], "dp", 1)
    extended = jnp.concatenate([head_rows, paired], axis=2)
    smoothed = short_taps(extended, short_filters, count)
    product = (smoothed[0] * smoothed[1]).astype(jnp.bfloat16)
    before = shifted(product[:, count - (taps - 1) :], "dp", 1)
    product_ext = jnp.concatenate([before, product], axis=1).reshape(seqs, span, groups, group_size)
    forward_band = band(medium_filters[:, ::-1], count)
    response = jnp.einsum(
        "gtr,srgm->stgm",
        forward_band,
        product_ext.astype(jnp.float32),
        precision=lax.Precision.HIGHEST,
    ).reshape(seqs, count, channels)
    position = lax.axis_index("dp") * count + jnp.arange(count, dtype=jnp.int32)
    live = (position[None, :] < lengths[:, None])[:, :, None]
    mixed = jnp.where(live, response, 0.0).astype(jnp.bfloat16)
    upstream = jnp.where(live, cotangent, jnp.zeros_like(cotangent))
    after = shifted(upstream[:, : taps - 1], "dp", -1)
    upstream_ext = jnp.concatenate([upstream, after], axis=1).reshape(
        seqs, span, groups, group_size
    )
    backward_band = band(medium_filters, count)
    product_grad = jnp.einsum(
        "gtr,srgm->stgm",
        backward_band,
        upstream_ext.astype(jnp.float32),
        precision=lax.Precision.HIGHEST,
    ).reshape(seqs, count, channels)
    correlation = jnp.einsum(
        "stgm,srgm->gtr",
        upstream.reshape(seqs, count, groups, group_size),
        product_ext,
        preferred_element_type=jnp.float32,
    )
    medium_local = band_sums(correlation, count, taps)
    smooth_grad = jnp.stack([product_grad * smoothed[1], product_grad * smoothed[0]])
    short_local = filter_terms(smooth_grad, extended, count, short_width)
    ahead_rows = shifted(smooth_grad[:, :, : short_width - 1], "dp", -1)
    pair_grad = short_ahead(
        jnp.concatenate([smooth_grad, ahead_rows], axis=2), short_filters, count
    )
    short_grad, medium_grad = lax.psum((short_local, medium_local), "dp")
    outgoing = (
        pair_grad.astype(jnp.bfloat16).transpose(1, 2, 0, 3).reshape(seqs * count, 2 * channels)
    )
    flat_features = features.reshape(seqs * count, -1)
    grads = lax.psum_scatter(
        lax.dot_general(
            flat_features, outgoing, (((0,), (0,)), ((), ())), preferred_element_type=jnp.float32
        ).astype(jnp.bfloat16),
        "dp",
        scatter_dimension=0,
        tiled=True,
    ).astype(jnp.float32)
    key_grad = grads[:, :channels].astype(jnp.bfloat16)
    value_grad = grads[:, channels:].astype(jnp.bfloat16)
    return (mixed, key_grad, value_grad, short_grad, medium_grad)


def hyena_kernel(
    taps,
    group,
    lengths_ref,
    keys_ref,
    values_ref,
    cot_ref,
    short_ref,
    medium_ref,
    reversed_ref,
    mixed_ref,
    act_ref,
    small_ref,
    pad_ref,
    smooth_ref,
    grad_ref,
    product_ref,
    upstream_ref,
    ahead_band,
    behind_band,
    corr_ref,
    short_acc,
):
    seqs, blocks, count, lanes = keys_ref.shape
    halves = count // BLOCK
    steps = blocks * halves
    length = blocks * count
    groups = lanes // group
    wide = seqs * lanes

    for g in range(groups):
        rows = pl.ds(g * BLOCK, BLOCK)
        base = jnp.broadcast_to(reversed_ref[g : g + 1, :], (BLOCK, 2 * BLOCK))
        behind_band[rows, :] = pltpu.roll(base, 0, 1, stride=1, stride_axis=0).astype(jnp.bfloat16)
        base = jnp.broadcast_to(medium_ref[g : g + 1, :], (BLOCK, 2 * BLOCK))
        ahead_band[rows, :] = pltpu.roll(base, 0, 1, stride=1, stride_axis=0).astype(jnp.bfloat16)

    zeros8 = jnp.zeros((8, lanes), jnp.float32)
    zeros_block = jnp.zeros((BLOCK, lanes), jnp.bfloat16)
    for s in range(seqs):
        for branch in range(2):
            pad_ref[branch, s, pl.ds(0, 8), :] = zeros8
            grad_ref[branch, s, pl.ds(length, 8), :] = zeros8
        product_ref[pl.ds(0, BLOCK), pl.ds(s * lanes, lanes)] = zeros_block
        upstream_ref[pl.ds(length, BLOCK), pl.ds(s * lanes, lanes)] = zeros_block

    def smooth(step, carry):
        block, half = step // halves, step % halves
        source = pl.ds(pl.multiple_of(half * BLOCK, BLOCK), BLOCK)
        begin = pl.multiple_of(step * BLOCK, BLOCK)
        place = lax.broadcasted_iota(jnp.int32, (BLOCK, lanes), 0) + begin
        for s in range(seqs):
            parts = []
            for branch, ref in ((0, keys_ref), (1, values_ref)):
                now = ref[s, block, source, :].astype(jnp.float32)
                pad_ref[branch, s, pl.ds(begin + 8, BLOCK), :] = now
                window = pad_ref[branch, s, pl.ds(begin, BLOCK + 8), :]
                total = short_ref[branch, 0:1, :] * now
                for tap in range(1, taps):
                    total += short_ref[branch, tap : tap + 1, :] * window[8 - tap : 8 - tap + BLOCK]
                smooth_ref[branch, s, pl.ds(begin, BLOCK), :] = total
                parts.append(total)
            columns = pl.ds(s * lanes, lanes)
            product_ref[pl.ds(begin + BLOCK, BLOCK), columns] = (parts[0] * parts[1]).astype(
                jnp.bfloat16
            )
            cot = cot_ref[block, s, source, :].astype(jnp.float32)
            upstream_ref[pl.ds(begin, BLOCK), columns] = jnp.where(
                place < lengths_ref[s], cot, 0.0
            ).astype(jnp.bfloat16)
        return carry

    lax.fori_loop(0, steps, smooth, 0)

    lane_group = lax.broadcasted_iota(jnp.int32, (BLOCK, wide), 1) % lanes // group
    corr_ref[...] = jnp.zeros_like(corr_ref)
    short_acc[...] = jnp.zeros_like(short_acc)

    def own(stacked):
        chosen = stacked[0:BLOCK]
        for g in range(1, groups):
            chosen = jnp.where(lane_group == g, stacked[g * BLOCK : (g + 1) * BLOCK], chosen)
        return chosen

    def mix(step, carry):
        block, half = step // halves, step % halves
        source = pl.ds(pl.multiple_of(half * BLOCK, BLOCK), BLOCK)
        begin = pl.multiple_of(step * BLOCK, BLOCK)
        place = lax.broadcasted_iota(jnp.int32, (BLOCK, lanes), 0) + begin
        past = product_ref[pl.ds(begin, 2 * BLOCK), :]
        response = own(jnp.dot(behind_band[...], past, preferred_element_type=jnp.float32))
        future = upstream_ref[pl.ds(begin, 2 * BLOCK), :]
        product_grad = own(jnp.dot(ahead_band[...], future, preferred_element_type=jnp.float32))
        here = future[0:BLOCK]
        apart = jnp.concatenate(
            [jnp.where(lane_group == g, here, jnp.zeros_like(here)) for g in range(groups)], axis=0
        )
        corr_ref[...] += lax.dot_general(
            apart, past, (((1,), (1,)), ((), ())), preferred_element_type=jnp.float32
        )
        for s in range(seqs):
            columns = slice(s * lanes, (s + 1) * lanes)
            mixed_ref[block, s, source, :] = jnp.where(
                place < lengths_ref[s], response[:, columns], 0.0
            ).astype(jnp.bfloat16)
            for branch in range(2):
                grad = product_grad[:, columns] * smooth_ref[1 - branch, s, pl.ds(begin, BLOCK), :]
                grad_ref[branch, s, pl.ds(begin, BLOCK), :] = grad
                window = pad_ref[branch, s, pl.ds(begin, BLOCK + 8), :]
                for tap in range(taps):
                    term = grad * window[8 - tap : 8 - tap + BLOCK]
                    short_acc[branch, tap] += jnp.sum(term.reshape(BLOCK // 8, 8, lanes), axis=0)
        return carry

    lax.fori_loop(0, steps, mix, 0)

    def back(step, carry):
        block, half = step // halves, step % halves
        source = pl.ds(pl.multiple_of(half * BLOCK, BLOCK), BLOCK)
        begin = pl.multiple_of(step * BLOCK, BLOCK)
        for s in range(seqs):
            for branch in range(2):
                window = grad_ref[branch, s, pl.ds(begin, BLOCK + 8), :]
                total = short_ref[branch, 0:1, :] * window[0:BLOCK]
                for tap in range(1, taps):
                    total += short_ref[branch, tap : tap + 1, :] * window[tap : tap + BLOCK]
                columns = slice(branch * lanes, (branch + 1) * lanes)
                act_ref[s, block, source, columns] = total.astype(jnp.bfloat16)
        return carry

    lax.fori_loop(0, steps, back, 0)

    for branch in range(2):
        for tap in range(8):
            if tap < taps:
                sums = jnp.sum(short_acc[branch, tap], axis=0, keepdims=True)
            else:
                sums = jnp.zeros((1, lanes), jnp.float32)
            small_ref[branch * 8 + tap : branch * 8 + tap + 1, :] = sums
    for g in range(groups):
        rows = BLOCK
        total = corr_ref[pl.ds(g * BLOCK, BLOCK), :]
        while rows > 1:
            rows //= 2
            total = total[:rows] + pltpu.roll(total[rows:], 2 * BLOCK - rows, 1)
        small_ref[16 + g : 17 + g, :] = total[:, :BLOCK]
        small_ref[16 + groups + g : 17 + groups + g, :] = total[:, BLOCK:]


def hyena(keys, values, cotangent, short_filters, medium_filters, lengths):
    seqs, blocks, count, lanes = keys.shape
    groups, medium = medium_filters.shape
    taps = short_filters.shape[-1]
    length = blocks * count
    short = jnp.pad(short_filters.transpose(0, 2, 1), ((0, 0), (0, 8 - taps), (0, 0)))
    forward = jnp.pad(medium_filters, ((0, 0), (0, 2 * BLOCK - medium)))
    backward = jnp.pad(
        medium_filters[:, ::-1], ((0, 0), (BLOCK + 1 - medium, BLOCK - 1))
    )
    vmem = pl.BlockSpec(memory_space=pltpu.VMEM)
    return pl.pallas_call(
        functools.partial(hyena_kernel, taps, lanes // groups),
        out_shape=(
            jax.ShapeDtypeStruct(cotangent.shape, jnp.bfloat16),
            jax.ShapeDtypeStruct((seqs, blocks, count, 2 * lanes), jnp.bfloat16),
            jax.ShapeDtypeStruct((16 + 2 * groups, lanes), jnp.float32),
        ),
        in_specs=[pl.BlockSpec(memory_space=pltpu.SMEM)] + [vmem] * 6,
        out_specs=[vmem] * 3,
        scratch_shapes=[
            pltpu.VMEM((2, seqs, length + 8, lanes), jnp.float32),
            pltpu.VMEM((2, seqs, length, lanes), jnp.float32),
            pltpu.VMEM((2, seqs, length + 8, lanes), jnp.float32),
            pltpu.VMEM((length + BLOCK, seqs * lanes), jnp.bfloat16),
            pltpu.VMEM((length + BLOCK, seqs * lanes), jnp.bfloat16),
            pltpu.VMEM((groups * BLOCK, 2 * BLOCK), jnp.bfloat16),
            pltpu.VMEM((groups * BLOCK, 2 * BLOCK), jnp.bfloat16),
            pltpu.VMEM((groups * BLOCK, 2 * BLOCK), jnp.float32),
            pltpu.VMEM((2, taps, 8, lanes), jnp.float32),
        ],
        compiler_params=pltpu.CompilerParams(vmem_limit_bytes=40 * 1024 * 1024),
        cost_estimate=pl.CostEstimate(
            flops=12 * groups * length * seqs * 2 * BLOCK * lanes,
            bytes_accessed=12 * length * seqs * lanes,
            transcendentals=0,
        ),
    )(lengths, keys, values, cotangent, short, forward, backward)


def remote(source, target, send, recv, dp, shard):
    return pltpu.make_async_remote_copy(
        src_ref=source,
        dst_ref=target,
        send_sem=send,
        recv_sem=recv,
        device_id={"dp": dp, "shard": shard},
        device_id_type=pl.DeviceIdType.MESH,
    )


def front_kernel(
    x_ref,
    key_ref,
    value_ref,
    cot_ref,
    keys_ref,
    values_ref,
    cot_out,
    features_out,
    line,
    features,
    panels,
    own,
    outgoing,
    incoming,
    cot_in,
    line_send,
    line_recv,
    plane_send,
    plane_recv,
    core_send,
    core_recv,
    sum_send,
    sum_recv,
    cot_send,
    cot_recv,
    local,
    saved,
):
    seqs, count, width = x_ref.shape
    blocks, lanes = cot_in.shape[0], cot_in.shape[-1]
    rows = count // 2
    p, shard = lax.axis_index("dp"), lax.axis_index("shard")
    z, core = shard // 2, shard % 2
    sibling = z * 2 + (1 - core)
    peers = [(p + j) % blocks for j in range(blocks)]
    froms = [(p + blocks - j) % blocks for j in range(blocks)]

    barrier = pltpu.get_barrier_semaphore()

    def greet(dp, to):
        pl.semaphore_signal(
            barrier,
            inc=1,
            device_id={"dp": dp, "shard": to},
            device_id_type=pl.DeviceIdType.MESH,
        )

    greet(p, sibling)
    for j in range(1, blocks):
        greet(peers[j], shard)

    for step in (2, 2 * blocks - 2):
        greet(p, (shard + step) % (2 * blocks))
    pl.semaphore_wait(barrier, blocks + 2)

    def part(half):
        return pl.ds(half * rows, rows)

    def held(h, layer, w, half):
        return x_ref.at[w, part(half)] if h == 0 else line.at[layer, w, part(half)]

    def line_copy(h, layer, w, half, way):
        piece = w * 2 + half
        return remote(
            held(h, layer, w, half),
            line.at[layer, w, part(half)],
            line_send.at[way, layer, piece],
            line_recv.at[layer, piece],
            p,
            shard + 2 * (1 - 2 * way),
        )

    def plane_copy(h, layer, w, half):
        piece = w * 2 + half
        return remote(
            held(h, layer, w, half),
            features.at[core, w, p, part(half)],
            plane_send.at[layer, piece],
            plane_recv.at[p, piece],
            layer,
            shard,
        )

    def plane_arrival(block, w, half):
        piece = w * 2 + half
        place = features.at[core, w, block, part(half)]
        return remote(
            place, place, plane_send.at[block, piece], plane_recv.at[block, piece], block, shard
        )

    def core_copy(source, block, w, half):
        piece = w * 2 + half
        return remote(
            source,
            features.at[core, w, block, part(half)],
            core_send.at[block, piece],
            core_recv.at[block, piece],
            p,
            sibling,
        )

    def core_arrival(block, w, half):
        piece = w * 2 + half
        place = features.at[1 - core, w, block, part(half)]
        return remote(
            place, place, core_send.at[block, piece], core_recv.at[block, piece], p, sibling
        )

    def keep_copy(h, layer, w, half):
        return pltpu.make_async_copy(
            held(h, layer, w, half), features.at[core, w, p, part(half)], local.at[w * 2 + half]
        )

    def steps(h):
        if h == 0:
            return [(0, z, None, z < blocks - 1), (1, z, None, z > 0)]
        return [
            (0, z - h, z - h >= 0, z < blocks - 1),
            (1, z + h, z + h < blocks, z > 0),
        ]

    def dispatch(h, layer, w, half):
        @pl.when(layer == p)
        def _():
            keep_copy(h, layer, w, half).start()
            core_copy(held(h, layer, w, half), p, w, half).start()

        @pl.when(layer != p)
        def _():
            plane_copy(h, layer, w, half).start()

    def hop(w, h):
        for half in range(2):
            if h == 0:
                for way, layer, _, onward in steps(0):

                    @pl.when(onward)
                    def _():
                        line_copy(0, layer, w, half, way).start()

                dispatch(0, z, w, half)
            else:
                for way, layer, valid, onward in steps(h):

                    @pl.when(valid)
                    def _():
                        line_copy(h, layer, w, half, way).wait_recv()

                        @pl.when(onward)
                        def _():
                            line_copy(h, layer, w, half, way).start()

                        dispatch(h, layer, w, half)

    def share(w):
        for half in range(2):
            for j in range(1, blocks):
                plane_arrival(froms[j], w, half).wait_recv()
                place = features.at[core, w, froms[j], part(half)]
                core_copy(place, froms[j], w, half).start()

    def save_copy(w):
        return pltpu.make_async_copy(features.at[:, w], features_out.at[:, w], saved.at[w])

    def complete(w):
        for half in range(2):
            for j in range(blocks):
                core_arrival(froms[j], w, half).wait_recv()
            keep_copy(0, z, w, half).wait()
        save_copy(w).start()

    def sum_copy(w, j):
        return remote(
            outgoing.at[w, j - 1],
            incoming.at[w, j - 1],
            sum_send.at[w, j - 1],
            sum_recv.at[w, j - 1],
            peers[j],
            shard,
        )

    def project(w, j):
        def tile(i, carry):
            total = jnp.zeros((count, 2 * lanes), jnp.float32)
            for c in range(2):
                total += jnp.dot(
                    features[c, w, i], panels[peers[j], c], preferred_element_type=jnp.float32
                )
            if j == 0:
                own[w, i] = total
            else:
                outgoing[w, j - 1, i] = total.astype(jnp.bfloat16)
            return carry

        lax.fori_loop(0, blocks, tile, 0)
        if j > 0:
            sum_copy(w, j).start()

    def cot_copy(j):
        place = pl.ds(pl.multiple_of(peers[j] * lanes, lanes), lanes)
        return remote(
            cot_ref.at[:, :, place],
            cot_in.at[p],
            cot_send.at[j],
            cot_recv.at[p],
            peers[j],
            shard,
        )

    def cot_arrival(j):
        return remote(
            cot_in.at[froms[j]],
            cot_in.at[froms[j]],
            cot_send.at[j],
            cot_recv.at[froms[j]],
            froms[j],
            shard,
        )

    hop(0, 0)
    for r in range(blocks):
        for c in range(2):
            source = pl.ds(c * width, width)
            columns = slice(r * lanes, (r + 1) * lanes)
            panels[r, c, :, 0:lanes] = key_ref[source, columns]
            panels[r, c, :, lanes : 2 * lanes] = value_ref[source, columns]
    for h in range(1, blocks):
        hop(0, h)
    hop(1, 0)
    share(0)
    hop(1, 1)
    complete(0)
    project(0, 2)
    project(0, 1)
    hop(1, 2)
    project(0, 3)
    hop(1, 3)
    project(0, 0)
    share(1)
    for j in range(1, blocks):
        cot_copy(j).start()
    cot_in[p] = cot_ref[:, :, pl.ds(pl.multiple_of(p * lanes, lanes), lanes)]
    complete(1)
    for j in (1, 3, 2, 0):
        project(1, j)
    for j in range(1, blocks):
        cot_arrival(j).wait_recv()
    cot_out[...] = cot_in[...]
    for w in range(seqs):
        for j in range(1, blocks):
            sum_copy(w, j).wait_recv()

        def add(i, carry):
            total = own[w, i]
            for j in range(1, blocks):
                total += incoming[w, j - 1, i].astype(jnp.float32)
            keys_ref[w, i] = total[:, 0:lanes].astype(jnp.bfloat16)
            values_ref[w, i] = total[:, lanes : 2 * lanes].astype(jnp.bfloat16)
            return carry

        lax.fori_loop(0, blocks, add, 0)

    for w in range(seqs):
        save_copy(w).wait()
        for j in range(1, blocks):
            sum_copy(w, j).wait_send()
        for half in range(2):
            for j in range(blocks):
                core_copy(features.at[core, w, froms[j], part(half)], froms[j], w, half).wait_send()
            for h in range(blocks):
                for way, layer, valid, onward in steps(h):
                    if h > 0:
                        onward = jnp.logical_and(valid, onward)

                    @pl.when(onward)
                    def _():
                        line_copy(h, layer, w, half, way).wait_send()

                    if h > 0 or way == 0:
                        sent = layer != p
                        if h > 0:
                            sent = jnp.logical_and(valid, sent)

                        @pl.when(sent)
                        def _():
                            plane_copy(h, layer, w, half).wait_send()

    for j in range(1, blocks):
        cot_copy(j).wait_send()


def front(inputs, key_panel, value_panel, cotangent, blocks):
    seqs, count, width = inputs.shape
    channels = key_panel.shape[1]
    lanes = channels // blocks
    pieces = 2 * seqs
    vmem = pl.BlockSpec(memory_space=pltpu.VMEM)
    hbm = pl.BlockSpec(memory_space=pl.ANY)
    acts = jax.ShapeDtypeStruct((seqs, blocks, count, lanes), jnp.bfloat16)
    feature_shape = (2, seqs, blocks, count, width)
    dma = pltpu.SemaphoreType.DMA
    return pl.pallas_call(
        front_kernel,
        out_shape=(
            acts,
            acts,
            jax.ShapeDtypeStruct((blocks, seqs, count, lanes), jnp.bfloat16),
            jax.ShapeDtypeStruct(feature_shape, jnp.bfloat16),
        ),
        in_specs=[hbm, vmem, vmem, vmem],
        out_specs=[vmem, vmem, vmem, hbm],
        scratch_shapes=[
            pltpu.VMEM((blocks, seqs, count, width), jnp.bfloat16),
            pltpu.VMEM(feature_shape, jnp.bfloat16),
            pltpu.VMEM((blocks, 2, width, 2 * lanes), jnp.bfloat16),
            pltpu.VMEM((seqs, blocks, count, 2 * lanes), jnp.float32),
            pltpu.VMEM((seqs, blocks - 1, blocks, count, 2 * lanes), jnp.bfloat16),
            pltpu.VMEM((seqs, blocks - 1, blocks, count, 2 * lanes), jnp.bfloat16),
            pltpu.VMEM((blocks, seqs, count, lanes), jnp.bfloat16),
            dma((2, blocks, pieces)),
            dma((blocks, pieces)),
            dma((blocks, pieces)),
            dma((blocks, pieces)),
            dma((blocks, pieces)),
            dma((blocks, pieces)),
            dma((seqs, blocks - 1)),
            dma((seqs, blocks - 1)),
            dma((blocks,)),
            dma((blocks,)),
            dma((pieces,)),
            dma((seqs,)),
        ],
        compiler_params=pltpu.CompilerParams(
            collective_id=0, has_side_effects=True, vmem_limit_bytes=48 * 1024 * 1024
        ),
        cost_estimate=pl.CostEstimate(
            flops=4 * blocks * seqs * count * 2 * width * channels,
            bytes_accessed=8 * blocks * seqs * count * width,
            transcendentals=0,
        ),
    )(inputs, key_panel, value_panel, cotangent)


def back_kernel(
    act_ref,
    mixed_ref,
    small_ref,
    features_ref,
    mixed_out,
    key_out,
    value_out,
    small_out,
    features,
    turned,
    got,
    mixed_in,
    small_in,
    act_send,
    act_recv,
    mixed_send,
    mixed_recv,
    small_send,
    small_recv,
    local,
):
    seqs, blocks, count, both = act_ref.shape
    lanes = both // 2
    width = features.shape[-1]
    p, shard = lax.axis_index("dp"), lax.axis_index("shard")
    x, y = p % 2, p // 2
    beside, above, across = y * 2 + 1 - x, (1 - y) * 2 + x, (1 - y) * 2 + 1 - x
    owners = (p, beside, above, across)

    loads = [
        pltpu.make_async_copy(features_ref.at[c], features.at[c], local.at[c]) for c in range(2)
    ]
    for load in loads:
        load.start()

    barrier = pltpu.get_barrier_semaphore()
    for to in owners[1:]:
        pl.semaphore_signal(
            barrier,
            inc=1,
            device_id={"dp": to, "shard": shard},
            device_id_type=pl.DeviceIdType.MESH,
        )
    pl.semaphore_wait(barrier, blocks - 1)

    def send_own(slot, w):
        return remote(
            act_ref.at[w],
            got.at[slot - 1, w],
            act_send.at[slot - 1, w],
            act_recv.at[slot - 1, w],
            owners[slot],
            shard,
        )

    def pass_on(slot, w):
        return remote(
            got.at[slot - 1, w],
            got.at[2, w],
            act_send.at[2, w],
            act_recv.at[2, w],
            owners[3 - slot],
            shard,
        )

    def arrived(slot, w):
        place = got.at[slot - 1, w]
        return remote(
            place,
            place,
            act_send.at[slot - 1, w],
            act_recv.at[slot - 1, w],
            owners[slot],
            shard,
        )

    def mixed_copy(k):
        return remote(
            mixed_ref.at[owners[k]],
            mixed_in.at[k - 1],
            mixed_send.at[k - 1],
            mixed_recv.at[k - 1],
            owners[k],
            shard,
        )

    def small_copy(k):
        return remote(
            small_ref,
            small_in.at[k - 1],
            small_send.at[k - 1],
            small_recv.at[k - 1],
            owners[k],
            shard,
        )

    send_own(1, 0).start()
    send_own(2, 1).start()
    send_own(1, 1).start()
    send_own(2, 0).start()
    for k in range(1, blocks):
        mixed_copy(k).start()
        small_copy(k).start()

    def turn(c):
        loads[c].wait()

        def tile(i, carry):
            w, block = i // blocks, i % blocks
            columns = pl.ds(pl.multiple_of(i * count, count), count)
            turned[c, :, columns] = features[c, w, block].T
            return carry

        lax.fori_loop(0, seqs * blocks, tile, 0)

    def grads(ref, owner):
        place = pl.ds(pl.multiple_of(owner * lanes, lanes), lanes)
        tall = width // 2

        def tile(i, carry):
            c, half = i // 2, i % 2
            rows = pl.ds(pl.multiple_of(half * tall, tall), tall)
            total = jnp.dot(
                turned[c, rows, :],
                ref[...].reshape(seqs * blocks * count, both),
                preferred_element_type=jnp.float32,
            ).astype(jnp.bfloat16)
            out = pl.ds(pl.multiple_of(i * tall, tall), tall)
            key_out[out, place] = total[:, :lanes]
            value_out[out, place] = total[:, lanes:]
            return carry

        lax.fori_loop(0, 4, tile, 0)

    turn(0)
    arrived(1, 0).wait_recv()
    pass_on(1, 0).start()
    arrived(2, 1).wait_recv()
    pass_on(2, 1).start()
    turn(1)
    grads(act_ref, p)
    arrived(1, 1).wait_recv()
    grads(got.at[0], beside)
    arrived(2, 0).wait_recv()
    grads(got.at[1], above)
    small_out[p] = small_ref[...]
    for k in range(1, blocks):
        small_copy(k).wait_recv()
        small_out[owners[k]] = small_in[k - 1]
    mixed_out[:, :, pl.ds(pl.multiple_of(p * lanes, lanes), lanes)] = mixed_ref[p]
    for k in range(1, blocks):
        mixed_copy(k).wait_recv()
        place = pl.ds(pl.multiple_of(owners[k] * lanes, lanes), lanes)
        mixed_out[:, :, place] = mixed_in[k - 1]
    for w in range(seqs):
        arrived(3, w).wait_recv()
    grads(got.at[2], across)
    for w in range(seqs):
        send_own(1, w).wait_send()
        send_own(2, w).wait_send()
        pass_on(1 + w, w).wait_send()
    for k in range(1, blocks):
        mixed_copy(k).wait_send()
        small_copy(k).wait_send()


def back(act, mixed, small, features):
    seqs, blocks, count, both = act.shape
    lanes = both // 2
    width = features.shape[-1]
    vmem = pl.BlockSpec(memory_space=pltpu.VMEM)
    dma = pltpu.SemaphoreType.DMA
    panel = jax.ShapeDtypeStruct((2 * width, blocks * lanes), jnp.bfloat16)
    return pl.pallas_call(
        back_kernel,
        out_shape=(
            jax.ShapeDtypeStruct((seqs, count, blocks * lanes), jnp.bfloat16),
            panel,
            panel,
            jax.ShapeDtypeStruct((blocks,) + small.shape, jnp.float32),
        ),
        in_specs=[vmem, vmem, vmem, pl.BlockSpec(memory_space=pl.ANY)],
        out_specs=[vmem] * 4,
        scratch_shapes=[
            pltpu.VMEM(features.shape, jnp.bfloat16),
            pltpu.VMEM((2, width, seqs * blocks * count), jnp.bfloat16),
            pltpu.VMEM((3,) + act.shape, jnp.bfloat16),
            pltpu.VMEM((blocks - 1,) + mixed.shape[1:], jnp.bfloat16),
            pltpu.VMEM((blocks - 1,) + small.shape, jnp.float32),
            dma((3, seqs)),
            dma((3, seqs)),
            dma((blocks - 1,)),
            dma((blocks - 1,)),
            dma((blocks - 1,)),
            dma((blocks - 1,)),
            dma((2,)),
        ],
        compiler_params=pltpu.CompilerParams(
            collective_id=1, has_side_effects=True, vmem_limit_bytes=48 * 1024 * 1024
        ),
        cost_estimate=pl.CostEstimate(
            flops=8 * seqs * blocks * count * width * blocks * lanes,
            bytes_accessed=4 * blocks * seqs * count * width,
            transcendentals=0,
        ),
    )(act, mixed, small, features)


def by_channels(inputs, key_panel, value_panel, short_filters, medium_filters, lengths, cotangent):
    seqs, count, width = inputs.shape
    blocks = lax.axis_size("dp")
    channels = key_panel.shape[1]
    lanes = channels // blocks
    groups = medium_filters.shape[0] // blocks
    mine = lax.axis_index("dp")
    keys, values, cot, features = front(inputs, key_panel, value_panel, cotangent, blocks)
    short = lax.dynamic_slice_in_dim(short_filters, mine * lanes, lanes, 1)
    medium = lax.dynamic_slice_in_dim(medium_filters, mine * groups, groups, 0)
    mixed, act, small = hyena(keys, values, cot, short, medium, lengths)
    mixed, key_grad, value_grad, small = back(act, mixed, small, features)
    taps, medium_taps = short_filters.shape[-1], medium_filters.shape[-1]
    short_grad = small[:, :16].reshape(blocks, 2, 8, lanes)[:, :, :taps]
    short_grad = short_grad.transpose(1, 0, 3, 2).reshape(2, channels, taps)
    sums = small[:, 16:].reshape(blocks, 2, groups, BLOCK).transpose(0, 2, 1, 3)
    sums = sums.reshape(blocks * groups, 2 * BLOCK)
    medium_grad = sums[:, BLOCK - medium_taps + 1 : BLOCK + 1][:, ::-1]
    return (mixed, key_grad, value_grad, short_grad, medium_grad)


def shards(inputs, key_panel, value_panel, short_filters, medium_filters, lengths, cotangent):
    blocks, shard = lax.axis_size("dp"), lax.axis_size("shard")
    channels = key_panel.shape[1]
    whole = channels == blocks * BLOCK and inputs.shape[1] % (2 * BLOCK) == 0
    plan = by_channels if whole and blocks == 4 and shard == 2 * blocks else by_positions
    return plan(
        inputs, key_panel, value_panel, short_filters, medium_filters, lengths, cotangent
    )


def solution(mesh):
    return jax.shard_map(
        shards,
        mesh=mesh,
        in_specs=(
            P(None, "dp", "shard"),
            P("dp", "shard"),
            P("dp", "shard"),
            P(None, "shard", None),
            P("shard", None),
            P(),
            P(None, "dp", "shard"),
        ),
        out_specs=(
            P(None, "dp", "shard"),
            P("dp", "shard"),
            P("dp", "shard"),
            P(None, "shard", None),
            P("shard", None),
        ),
        check_vma=False,
    )
```

```python
import functools

import jax
import jax.numpy as jnp
from jax import lax
from jax.experimental import pallas as pl
from jax.experimental.pallas import tpu as pltpu
from jax.sharding import PartitionSpec as P

BLOCK = 128


def shifted(value, axis, steps):
    count = lax.axis_size(axis)
    first, last = (max(0, -steps), min(count, count - steps))
    return lax.ppermute(value, axis, [(source, source + steps) for source in range(first, last)])


def band(filters, count):
    groups, taps = filters.shape
    width = count + taps - 1
    padded = jnp.concatenate([filters, jnp.zeros((groups, count), jnp.float32)], axis=1)
    tiled = jnp.tile(padded, (1, count))[:, : count * width]
    return tiled.reshape(groups, count, width)


def band_sums(correlation, count, taps):
    groups, _, width = correlation.shape
    flat = correlation.reshape(groups, count * width)
    padded = jnp.concatenate([flat, jnp.zeros((groups, count), jnp.float32)], axis=1)
    skewed = padded.reshape(groups, count, width + 1)
    return jnp.sum(skewed, axis=1)[:, :taps][:, ::-1]


def short_taps(extended, filters, count):
    width = filters.shape[-1]
    total = jnp.zeros(extended.shape[:2] + (count, extended.shape[3]), jnp.float32)
    for tap in range(width):
        begin = width - 1 - tap
        total = total + filters[:, None, None, :, tap] * extended[
            :, :, begin : begin + count
        ].astype(jnp.float32)
    return total


def short_ahead(extended, filters, count):
    width = filters.shape[-1]
    total = jnp.zeros(extended.shape[:2] + (count, extended.shape[3]), jnp.float32)
    for tap in range(width):
        total = total + filters[:, None, None, :, tap] * extended[:, :, tap : tap + count]
    return total


def filter_terms(grads, extended, count, width):
    columns = []
    for tap in range(width):
        begin = width - 1 - tap
        columns.append(
            jnp.sum(grads * extended[:, :, begin : begin + count].astype(jnp.float32), axis=(1, 2))
        )
    return jnp.stack(columns, axis=-1)


def by_positions(inputs, key_panel, value_panel, short_filters, medium_filters, lengths, cotangent):
    seqs, count, local_width = inputs.shape
    channels = key_panel.shape[1]
    groups, taps = medium_filters.shape
    group_size = channels // groups
    short_width = short_filters.shape[-1]
    span = count + taps - 1
    gathered = (
        lax.all_gather(key_panel, "dp", axis=0, tiled=True),
        lax.all_gather(value_panel, "dp", axis=0, tiled=True),
    )
    panels = jnp.concatenate([gathered[0], gathered[1]], axis=1)
    features = lax.all_gather(inputs, "shard", axis=2, tiled=True)
    projected = jnp.dot(
        features.reshape(seqs * count, -1), panels, preferred_element_type=jnp.float32
    )
    paired = projected.astype(jnp.bfloat16).reshape(seqs, count, 2, channels).transpose(2, 0, 1, 3)
    head_rows = shifted(paired[:, :, count - (short_width - 1) :], "dp", 1)
    extended = jnp.concatenate([head_rows, paired], axis=2)
    smoothed = short_taps(extended, short_filters, count)
    product = (smoothed[0] * smoothed[1]).astype(jnp.bfloat16)
    before = shifted(product[:, count - (taps - 1) :], "dp", 1)
    product_ext = jnp.concatenate([before, product], axis=1).reshape(seqs, span, groups, group_size)
    forward_band = band(medium_filters[:, ::-1], count)
    response = jnp.einsum(
        "gtr,srgm->stgm",
        forward_band,
        product_ext.astype(jnp.float32),
        precision=lax.Precision.HIGHEST,
    ).reshape(seqs, count, channels)
    position = lax.axis_index("dp") * count + jnp.arange(count, dtype=jnp.int32)
    live = (position[None, :] < lengths[:, None])[:, :, None]
    mixed = jnp.where(live, response, 0.0).astype(jnp.bfloat16)
    upstream = jnp.where(live, cotangent, jnp.zeros_like(cotangent))
    after = shifted(upstream[:, : taps - 1], "dp", -1)
    upstream_ext = jnp.concatenate([upstream, after], axis=1).reshape(
        seqs, span, groups, group_size
    )
    backward_band = band(medium_filters, count)
    product_grad = jnp.einsum(
        "gtr,srgm->stgm",
        backward_band,
        upstream_ext.astype(jnp.float32),
        precision=lax.Precision.HIGHEST,
    ).reshape(seqs, count, channels)
    correlation = jnp.einsum(
        "stgm,srgm->gtr",
        upstream.reshape(seqs, count, groups, group_size),
        product_ext,
        preferred_element_type=jnp.float32,
    )
    medium_local = band_sums(correlation, count, taps)
    smooth_grad = jnp.stack([product_grad * smoothed[1], product_grad * smoothed[0]])
    short_local = filter_terms(smooth_grad, extended, count, short_width)
    ahead_rows = shifted(smooth_grad[:, :, : short_width - 1], "dp", -1)
    pair_grad = short_ahead(
        jnp.concatenate([smooth_grad, ahead_rows], axis=2), short_filters, count
    )
    short_grad, medium_grad = lax.psum((short_local, medium_local), "dp")
    outgoing = (
        pair_grad.astype(jnp.bfloat16).transpose(1, 2, 0, 3).reshape(seqs * count, 2 * channels)
    )
    flat_features = features.reshape(seqs * count, -1)
    grads = lax.psum_scatter(
        lax.dot_general(
            flat_features, outgoing, (((0,), (0,)), ((), ())), preferred_element_type=jnp.float32
        ).astype(jnp.bfloat16),
        "dp",
        scatter_dimension=0,
        tiled=True,
    ).astype(jnp.float32)
    key_grad = grads[:, :channels].astype(jnp.bfloat16)
    value_grad = grads[:, channels:].astype(jnp.bfloat16)
    return (mixed, key_grad, value_grad, short_grad, medium_grad)


def hyena_kernel(
    taps,
    group,
    lengths_ref,
    keys_ref,
    values_ref,
    cot_ref,
    short_ref,
    medium_ref,
    reversed_ref,
    mixed_ref,
    act_ref,
    small_ref,
    pad_ref,
    smooth_ref,
    grad_ref,
    product_ref,
    upstream_ref,
    ahead_band,
    behind_band,
    corr_ref,
    short_acc,
):
    seqs, blocks, count, lanes = keys_ref.shape
    halves = count // BLOCK
    steps = blocks * halves
    length = blocks * count
    groups = lanes // group
    wide = seqs * lanes

    for g in range(groups):
        rows = pl.ds(g * BLOCK, BLOCK)
        base = jnp.broadcast_to(reversed_ref[g : g + 1, :], (BLOCK, 2 * BLOCK))
        behind_band[rows, :] = pltpu.roll(base, 0, 1, stride=1, stride_axis=0).astype(jnp.bfloat16)
        base = jnp.broadcast_to(medium_ref[g : g + 1, :], (BLOCK, 2 * BLOCK))
        ahead_band[rows, :] = pltpu.roll(base, 0, 1, stride=1, stride_axis=0).astype(jnp.bfloat16)

    zeros8 = jnp.zeros((8, lanes), jnp.float32)
    zeros_block = jnp.zeros((BLOCK, lanes), jnp.bfloat16)
    for s in range(seqs):
        for branch in range(2):
            pad_ref[branch, s, pl.ds(0, 8), :] = zeros8
            grad_ref[branch, s, pl.ds(length, 8), :] = zeros8
        product_ref[pl.ds(0, BLOCK), pl.ds(s * lanes, lanes)] = zeros_block
        upstream_ref[pl.ds(length, BLOCK), pl.ds(s * lanes, lanes)] = zeros_block

    def smooth(step, carry):
        block, half = step // halves, step % halves
        source = pl.ds(pl.multiple_of(half * BLOCK, BLOCK), BLOCK)
        begin = pl.multiple_of(step * BLOCK, BLOCK)
        place = lax.broadcasted_iota(jnp.int32, (BLOCK, lanes), 0) + begin
        for s in range(seqs):
            parts = []
            for branch, ref in ((0, keys_ref), (1, values_ref)):
                now = ref[s, block, source, :].astype(jnp.float32)
                pad_ref[branch, s, pl.ds(begin + 8, BLOCK), :] = now
                window = pad_ref[branch, s, pl.ds(begin, BLOCK + 8), :]
                total = short_ref[branch, 0:1, :] * now
                for tap in range(1, taps):
                    total += short_ref[branch, tap : tap + 1, :] * window[8 - tap : 8 - tap + BLOCK]
                smooth_ref[branch, s, pl.ds(begin, BLOCK), :] = total
                parts.append(total)
            columns = pl.ds(s * lanes, lanes)
            product_ref[pl.ds(begin + BLOCK, BLOCK), columns] = (parts[0] * parts[1]).astype(
                jnp.bfloat16
            )
            cot = cot_ref[block, s, source, :].astype(jnp.float32)
            upstream_ref[pl.ds(begin, BLOCK), columns] = jnp.where(
                place < lengths_ref[s], cot, 0.0
            ).astype(jnp.bfloat16)
        return carry

    lax.fori_loop(0, steps, smooth, 0)

    lane_group = lax.broadcasted_iota(jnp.int32, (BLOCK, wide), 1) % lanes // group
    corr_ref[...] = jnp.zeros_like(corr_ref)
    short_acc[...] = jnp.zeros_like(short_acc)

    def own(stacked):
        chosen = stacked[0:BLOCK]
        for g in range(1, groups):
            chosen = jnp.where(lane_group == g, stacked[g * BLOCK : (g + 1) * BLOCK], chosen)
        return chosen

    def mix(step, carry):
        block, half = step // halves, step % halves
        source = pl.ds(pl.multiple_of(half * BLOCK, BLOCK), BLOCK)
        begin = pl.multiple_of(step * BLOCK, BLOCK)
        place = lax.broadcasted_iota(jnp.int32, (BLOCK, lanes), 0) + begin
        past = product_ref[pl.ds(begin, 2 * BLOCK), :]
        response = own(jnp.dot(behind_band[...], past, preferred_element_type=jnp.float32))
        future = upstream_ref[pl.ds(begin, 2 * BLOCK), :]
        product_grad = own(jnp.dot(ahead_band[...], future, preferred_element_type=jnp.float32))
        here = future[0:BLOCK]
        apart = jnp.concatenate(
            [jnp.where(lane_group == g, here, jnp.zeros_like(here)) for g in range(groups)], axis=0
        )
        corr_ref[...] += lax.dot_general(
            apart, past, (((1,), (1,)), ((), ())), preferred_element_type=jnp.float32
        )
        for s in range(seqs):
            columns = slice(s * lanes, (s + 1) * lanes)
            mixed_ref[block, s, source, :] = jnp.where(
                place < lengths_ref[s], response[:, columns], 0.0
            ).astype(jnp.bfloat16)
            for branch in range(2):
                grad = product_grad[:, columns] * smooth_ref[1 - branch, s, pl.ds(begin, BLOCK), :]
                grad_ref[branch, s, pl.ds(begin, BLOCK), :] = grad
                window = pad_ref[branch, s, pl.ds(begin, BLOCK + 8), :]
                for tap in range(taps):
                    term = grad * window[8 - tap : 8 - tap + BLOCK]
                    short_acc[branch, tap] += jnp.sum(term.reshape(BLOCK // 8, 8, lanes), axis=0)
        return carry

    lax.fori_loop(0, steps, mix, 0)

    def back(step, carry):
        block, half = step // halves, step % halves
        source = pl.ds(pl.multiple_of(half * BLOCK, BLOCK), BLOCK)
        begin = pl.multiple_of(step * BLOCK, BLOCK)
        for s in range(seqs):
            for branch in range(2):
                window = grad_ref[branch, s, pl.ds(begin, BLOCK + 8), :]
                total = short_ref[branch, 0:1, :] * window[0:BLOCK]
                for tap in range(1, taps):
                    total += short_ref[branch, tap : tap + 1, :] * window[tap : tap + BLOCK]
                columns = slice(branch * lanes, (branch + 1) * lanes)
                act_ref[s, block, source, columns] = total.astype(jnp.bfloat16)
        return carry

    lax.fori_loop(0, steps, back, 0)

    for branch in range(2):
        for tap in range(8):
            if tap < taps:
                sums = jnp.sum(short_acc[branch, tap], axis=0, keepdims=True)
            else:
                sums = jnp.zeros((1, lanes), jnp.float32)
            small_ref[branch * 8 + tap : branch * 8 + tap + 1, :] = sums
    for g in range(groups):
        rows = BLOCK
        total = corr_ref[pl.ds(g * BLOCK, BLOCK), :]
        while rows > 1:
            rows //= 2
            total = total[:rows] + pltpu.roll(total[rows:], 2 * BLOCK - rows, 1)
        small_ref[16 + g : 17 + g, :] = total[:, :BLOCK]
        small_ref[16 + groups + g : 17 + groups + g, :] = total[:, BLOCK:]


def hyena(keys, values, cotangent, short_filters, medium_filters, lengths):
    seqs, blocks, count, lanes = keys.shape
    groups, medium = medium_filters.shape
    taps = short_filters.shape[-1]
    length = blocks * count
    short = jnp.pad(short_filters.transpose(0, 2, 1), ((0, 0), (0, 8 - taps), (0, 0)))
    forward = jnp.pad(medium_filters, ((0, 0), (0, 2 * BLOCK - medium)))
    backward = jnp.pad(
        medium_filters[:, ::-1], ((0, 0), (BLOCK + 1 - medium, BLOCK - 1))
    )
    vmem = pl.BlockSpec(memory_space=pltpu.VMEM)
    return pl.pallas_call(
        functools.partial(hyena_kernel, taps, lanes // groups),
        out_shape=(
            jax.ShapeDtypeStruct(cotangent.shape, jnp.bfloat16),
            jax.ShapeDtypeStruct((seqs, blocks, count, 2 * lanes), jnp.bfloat16),
            jax.ShapeDtypeStruct((16 + 2 * groups, lanes), jnp.float32),
        ),
        in_specs=[pl.BlockSpec(memory_space=pltpu.SMEM)] + [vmem] * 6,
        out_specs=[vmem] * 3,
        scratch_shapes=[
            pltpu.VMEM((2, seqs, length + 8, lanes), jnp.float32),
            pltpu.VMEM((2, seqs, length, lanes), jnp.float32),
            pltpu.VMEM((2, seqs, length + 8, lanes), jnp.float32),
            pltpu.VMEM((length + BLOCK, seqs * lanes), jnp.bfloat16),
            pltpu.VMEM((length + BLOCK, seqs * lanes), jnp.bfloat16),
            pltpu.VMEM((groups * BLOCK, 2 * BLOCK), jnp.bfloat16),
            pltpu.VMEM((groups * BLOCK, 2 * BLOCK), jnp.bfloat16),
            pltpu.VMEM((groups * BLOCK, 2 * BLOCK), jnp.float32),
            pltpu.VMEM((2, taps, 8, lanes), jnp.float32),
        ],
        compiler_params=pltpu.CompilerParams(vmem_limit_bytes=40 * 1024 * 1024),
        cost_estimate=pl.CostEstimate(
            flops=12 * groups * length * seqs * 2 * BLOCK * lanes,
            bytes_accessed=12 * length * seqs * lanes,
            transcendentals=0,
        ),
    )(lengths, keys, values, cotangent, short, forward, backward)


def remote(source, target, send, recv, dp, shard):
    return pltpu.make_async_remote_copy(
        src_ref=source,
        dst_ref=target,
        send_sem=send,
        recv_sem=recv,
        device_id={"dp": dp, "shard": shard},
        device_id_type=pl.DeviceIdType.MESH,
    )


def front_kernel(
    x_ref,
    key_ref,
    value_ref,
    cot_ref,
    keys_ref,
    values_ref,
    cot_out,
    features_out,
    line,
    features,
    panels,
    own,
    outgoing,
    incoming,
    cot_in,
    line_send,
    line_recv,
    plane_send,
    plane_recv,
    core_send,
    core_recv,
    sum_send,
    sum_recv,
    cot_send,
    cot_recv,
    local,
    saved,
    panel_sem,
    cot_local,
):
    seqs, count, width = x_ref.shape
    blocks, lanes = cot_in.shape[0], cot_in.shape[-1]
    rows = count // 2
    chunks = 2 * seqs
    p, shard = lax.axis_index("dp"), lax.axis_index("shard")
    z, core = shard // 2, shard % 2
    sibling = z * 2 + (1 - core)
    peers = [(p + j) % blocks for j in range(blocks)]
    froms = [(p + blocks - j) % blocks for j in range(blocks)]

    barrier = pltpu.get_barrier_semaphore()

    def greet(dp, to):
        pl.semaphore_signal(
            barrier,
            inc=1,
            device_id={"dp": dp, "shard": to},
            device_id_type=pl.DeviceIdType.MESH,
        )

    greet(p, sibling)
    for j in range(1, blocks):
        greet(peers[j], shard)

    for step in (2, 2 * blocks - 2):
        greet(p, (shard + step) % (2 * blocks))
    pl.semaphore_wait(barrier, blocks + 2)

    def block_of(k):
        return x_ref.at[k // 2, pl.ds(k % 2 * rows, rows)]

    def held(h, layer, k):
        return block_of(k) if h == 0 else line.at[layer, k]

    def line_copy(h, layer, k, way):
        return remote(
            held(h, layer, k),
            line.at[layer, k],
            line_send.at[way, layer, k],
            line_recv.at[layer, k],
            p,
            shard + 2 * (1 - 2 * way),
        )

    def plane_copy(h, layer, k):
        return remote(
            held(h, layer, k),
            features.at[core, k, p],
            plane_send.at[layer, k],
            plane_recv.at[p, k],
            layer,
            shard,
        )

    def plane_arrival(block, k):
        place = features.at[core, k, block]
        return remote(
            place, place, plane_send.at[block, k], plane_recv.at[block, k], block, shard
        )

    def core_copy(source, block, k):
        return remote(
            source,
            features.at[core, k, block],
            core_send.at[block, k],
            core_recv.at[block, k],
            p,
            sibling,
        )

    def core_arrival(block, k):
        place = features.at[1 - core, k, block]
        return remote(place, place, core_send.at[block, k], core_recv.at[block, k], p, sibling)

    def keep_copy(h, layer, k):
        return pltpu.make_async_copy(held(h, layer, k), features.at[core, k, p], local.at[k])

    def steps(h):
        if h == 0:
            return [(0, z, None, z < blocks - 1), (1, z, None, z > 0)]
        return [
            (0, z - h, z - h >= 0, z < blocks - 1),
            (1, z + h, z + h < blocks, z > 0),
        ]

    def dispatch(h, layer, k):
        @pl.when(layer == p)
        def _():
            keep_copy(h, layer, k).start()
            core_copy(held(h, layer, k), p, k).start()

        @pl.when(layer != p)
        def _():
            plane_copy(h, layer, k).start()

    def hop(k, h):
        if h == 0:
            for way, layer, _, onward in steps(0):

                @pl.when(onward)
                def _():
                    line_copy(0, layer, k, way).start()

            dispatch(0, z, k)
            return
        for way, layer, valid, onward in steps(h):

            @pl.when(valid)
            def _():
                line_copy(h, layer, k, way).wait_recv()

                @pl.when(onward)
                def _():
                    line_copy(h, layer, k, way).start()

                dispatch(h, layer, k)

    def share(k):
        for j in range(1, blocks):
            plane_arrival(froms[j], k).wait_recv()
            core_copy(features.at[core, k, froms[j]], froms[j], k).start()

    def save_copy(k):
        return pltpu.make_async_copy(features.at[:, k], features_out.at[:, k], saved.at[k])

    def complete(k):
        for j in range(blocks):
            core_arrival(froms[j], k).wait_recv()
        keep_copy(0, z, k).wait()
        save_copy(k).start()

    def sum_copy(k, j):
        return remote(
            outgoing.at[k, j - 1],
            incoming.at[k, j - 1],
            sum_send.at[k, j - 1],
            sum_recv.at[k, j - 1],
            (p + j) % blocks,
            shard,
        )

    def product(k, owner):
        total = jnp.zeros((blocks * rows, 2 * lanes), jnp.float32)
        for c in range(2):
            total += jnp.dot(
                features[c, k].reshape(blocks * rows, width),
                panels[owner, c],
                preferred_element_type=jnp.float32,
            )
        return total

    def project(k):
        def others(j, carry):
            outgoing[k, j - 1] = product(k, (p + j) % blocks).astype(jnp.bfloat16)
            sum_copy(k, j).start()
            return carry

        lax.fori_loop(1, blocks, others, 0)
        own[k] = product(k, p)

    def cot_place(owner):
        return pl.ds(pl.multiple_of(owner * lanes, lanes), lanes)

    def cot_copy(j):
        return remote(
            cot_ref.at[:, :, cot_place(peers[j])],
            cot_in.at[p],
            cot_send.at[j],
            cot_recv.at[p],
            peers[j],
            shard,
        )

    def cot_arrival(j):
        place = cot_in.at[froms[j]]
        return remote(place, place, cot_send.at[j], cot_recv.at[froms[j]], froms[j], shard)

    cot_keep = pltpu.make_async_copy(
        cot_ref.at[:, :, cot_place(p)], cot_in.at[p], cot_local.at[0]
    )
    panel_copies = [
        pltpu.make_async_copy(
            ref.at[pl.ds(c * width, width), pl.ds(r * lanes, lanes)],
            panels.at[r, c, :, pl.ds(branch * lanes, lanes)],
            panel_sem.at[branch, r, c],
        )
        for branch, ref in ((0, key_ref), (1, value_ref))
        for r in range(blocks)
        for c in range(2)
    ]

    hop(0, 0)
    for j in range(1, blocks):
        cot_copy(j).start()
    cot_keep.start()
    for copy in panel_copies:
        copy.start()
    hop(0, 1)
    hop(0, 2)
    hop(1, 0)
    hop(0, 3)
    for k in range(1, chunks):
        hop(k, 1)
        hop(k, 2)
        if k + 1 < chunks:
            hop(k + 1, 0)
        share(k - 1)
        hop(k, 3)
        complete(k - 1)
        if k == 1:
            for copy in panel_copies:
                copy.wait()
        project(k - 1)
    share(chunks - 1)
    cot_keep.wait()
    for j in range(1, blocks):
        cot_arrival(j).wait_recv()
    cot_out[...] = cot_in[...]
    complete(chunks - 1)
    project(chunks - 1)
    for k in range(chunks):
        for j in range(1, blocks):
            sum_copy(k, j).wait_recv()
        total = own[k]
        for j in range(1, blocks):
            total += incoming[k, j - 1].astype(jnp.float32)
        total = total.astype(jnp.bfloat16).reshape(blocks, rows, 2 * lanes)
        place = pl.ds(k % 2 * rows, rows)
        keys_ref[k // 2, :, place, :] = total[:, :, 0:lanes]
        values_ref[k // 2, :, place, :] = total[:, :, lanes : 2 * lanes]

    for k in range(chunks):
        save_copy(k).wait()
        for j in range(1, blocks):
            sum_copy(k, j).wait_send()
        for j in range(blocks):
            core_copy(features.at[core, k, froms[j]], froms[j], k).wait_send()
        for h in range(blocks):
            for way, layer, valid, onward in steps(h):
                if h > 0:
                    onward = jnp.logical_and(valid, onward)

                @pl.when(onward)
                def _():
                    line_copy(h, layer, k, way).wait_send()

                if h > 0 or way == 0:
                    sent = layer != p
                    if h > 0:
                        sent = jnp.logical_and(valid, sent)

                    @pl.when(sent)
                    def _():
                        plane_copy(h, layer, k).wait_send()

    for j in range(1, blocks):
        cot_copy(j).wait_send()


def front(inputs, key_panel, value_panel, cotangent, blocks):
    seqs, count, width = inputs.shape
    channels = key_panel.shape[1]
    lanes = channels // blocks
    pieces = 2 * seqs
    vmem = pl.BlockSpec(memory_space=pltpu.VMEM)
    hbm = pl.BlockSpec(memory_space=pl.ANY)
    acts = jax.ShapeDtypeStruct((seqs, blocks, count, lanes), jnp.bfloat16)
    feature_shape = (2, pieces, blocks, count // 2, width)
    tall = blocks * count // 2
    dma = pltpu.SemaphoreType.DMA
    return pl.pallas_call(
        front_kernel,
        out_shape=(
            acts,
            acts,
            jax.ShapeDtypeStruct((blocks, seqs, count, lanes), jnp.bfloat16),
            jax.ShapeDtypeStruct(feature_shape, jnp.bfloat16),
        ),
        in_specs=[hbm] * 4,
        out_specs=[vmem, vmem, vmem, hbm],
        scratch_shapes=[
            pltpu.VMEM((blocks, pieces, count // 2, width), jnp.bfloat16),
            pltpu.VMEM(feature_shape, jnp.bfloat16),
            pltpu.VMEM((blocks, 2, width, 2 * lanes), jnp.bfloat16),
            pltpu.VMEM((pieces, tall, 2 * lanes), jnp.float32),
            pltpu.VMEM((pieces, blocks - 1, tall, 2 * lanes), jnp.bfloat16),
            pltpu.VMEM((pieces, blocks - 1, tall, 2 * lanes), jnp.bfloat16),
            pltpu.VMEM((blocks, seqs, count, lanes), jnp.bfloat16),
            dma((2, blocks, pieces)),
            dma((blocks, pieces)),
            dma((blocks, pieces)),
            dma((blocks, pieces)),
            dma((blocks, pieces)),
            dma((blocks, pieces)),
            dma((pieces, blocks - 1)),
            dma((pieces, blocks - 1)),
            dma((blocks,)),
            dma((blocks,)),
            dma((pieces,)),
            dma((pieces,)),
            dma((2, blocks, 2)),
            dma((1,)),
        ],
        compiler_params=pltpu.CompilerParams(
            collective_id=0, has_side_effects=True, vmem_limit_bytes=48 * 1024 * 1024
        ),
        cost_estimate=pl.CostEstimate(
            flops=4 * blocks * seqs * count * 2 * width * channels,
            bytes_accessed=8 * blocks * seqs * count * width,
            transcendentals=0,
        ),
    )(inputs, key_panel, value_panel, cotangent)


def back_kernel(
    act_ref,
    mixed_ref,
    small_ref,
    features_ref,
    mixed_out,
    key_out,
    value_out,
    small_out,
    features,
    turned,
    got,
    mixed_in,
    small_in,
    act_send,
    act_recv,
    mixed_send,
    mixed_recv,
    small_send,
    small_recv,
    local,
):
    seqs, blocks, count, both = act_ref.shape
    lanes = both // 2
    width = features.shape[-1]
    p, shard = lax.axis_index("dp"), lax.axis_index("shard")
    x, y = p % 2, p // 2
    beside, above, across = y * 2 + 1 - x, (1 - y) * 2 + x, (1 - y) * 2 + 1 - x
    owners = (p, beside, above, across)

    loads = [
        pltpu.make_async_copy(features_ref.at[c], features.at[c], local.at[c]) for c in range(2)
    ]
    for load in loads:
        load.start()

    barrier = pltpu.get_barrier_semaphore()
    for to in owners[1:]:
        pl.semaphore_signal(
            barrier,
            inc=1,
            device_id={"dp": to, "shard": shard},
            device_id_type=pl.DeviceIdType.MESH,
        )
    pl.semaphore_wait(barrier, blocks - 1)

    def send_own(slot, w):
        return remote(
            act_ref.at[w],
            got.at[slot - 1, w],
            act_send.at[slot - 1, w],
            act_recv.at[slot - 1, w],
            owners[slot],
            shard,
        )

    def pass_on(slot, w):
        return remote(
            got.at[slot - 1, w],
            got.at[2, w],
            act_send.at[2, w],
            act_recv.at[2, w],
            owners[3 - slot],
            shard,
        )

    def arrived(slot, w):
        place = got.at[slot - 1, w]
        return remote(
            place,
            place,
            act_send.at[slot - 1, w],
            act_recv.at[slot - 1, w],
            owners[slot],
            shard,
        )

    def mixed_copy(k):
        return remote(
            mixed_ref.at[owners[k]],
            mixed_in.at[k - 1],
            mixed_send.at[k - 1],
            mixed_recv.at[k - 1],
            owners[k],
            shard,
        )

    def small_copy(k):
        return remote(
            small_ref,
            small_in.at[k - 1],
            small_send.at[k - 1],
            small_recv.at[k - 1],
            owners[k],
            shard,
        )

    send_own(1, 0).start()
    send_own(2, 1).start()
    send_own(1, 1).start()
    send_own(2, 0).start()
    for k in range(1, blocks):
        mixed_copy(k).start()
        small_copy(k).start()

    def turn(c):
        loads[c].wait()

        def tile(i, carry):
            k, block = i // blocks, i % blocks
            rows = count // 2
            begin = ((k // 2 * blocks + block) * 2 + k % 2) * rows
            columns = pl.ds(pl.multiple_of(begin, rows), rows)
            turned[c, :, columns] = features[c, k, block].T
            return carry

        lax.fori_loop(0, 2 * seqs * blocks, tile, 0)

    def grads(ref, owner):
        place = pl.ds(pl.multiple_of(owner * lanes, lanes), lanes)
        tall = width // 2

        def tile(i, carry):
            c, half = i // 2, i % 2
            rows = pl.ds(pl.multiple_of(half * tall, tall), tall)
            total = jnp.dot(
                turned[c, rows, :],
                ref[...].reshape(seqs * blocks * count, both),
                preferred_element_type=jnp.float32,
            ).astype(jnp.bfloat16)
            out = pl.ds(pl.multiple_of(i * tall, tall), tall)
            key_out[out, place] = total[:, :lanes]
            value_out[out, place] = total[:, lanes:]
            return carry

        lax.fori_loop(0, 4, tile, 0)

    turn(0)
    arrived(1, 0).wait_recv()
    pass_on(1, 0).start()
    arrived(2, 1).wait_recv()
    pass_on(2, 1).start()
    turn(1)
    grads(act_ref, p)
    arrived(1, 1).wait_recv()
    grads(got.at[0], beside)
    arrived(2, 0).wait_recv()
    grads(got.at[1], above)
    small_out[p] = small_ref[...]
    for k in range(1, blocks):
        small_copy(k).wait_recv()
        small_out[owners[k]] = small_in[k - 1]
    mixed_out[:, :, pl.ds(pl.multiple_of(p * lanes, lanes), lanes)] = mixed_ref[p]
    for k in range(1, blocks):
        mixed_copy(k).wait_recv()
        place = pl.ds(pl.multiple_of(owners[k] * lanes, lanes), lanes)
        mixed_out[:, :, place] = mixed_in[k - 1]
    for w in range(seqs):
        arrived(3, w).wait_recv()
    grads(got.at[2], across)
    for w in range(seqs):
        send_own(1, w).wait_send()
        send_own(2, w).wait_send()
        pass_on(1 + w, w).wait_send()
    for k in range(1, blocks):
        mixed_copy(k).wait_send()
        small_copy(k).wait_send()


def back(act, mixed, small, features):
    seqs, blocks, count, both = act.shape
    lanes = both // 2
    width = features.shape[-1]
    vmem = pl.BlockSpec(memory_space=pltpu.VMEM)
    dma = pltpu.SemaphoreType.DMA
    panel = jax.ShapeDtypeStruct((2 * width, blocks * lanes), jnp.bfloat16)
    return pl.pallas_call(
        back_kernel,
        out_shape=(
            jax.ShapeDtypeStruct((seqs, count, blocks * lanes), jnp.bfloat16),
            panel,
            panel,
            jax.ShapeDtypeStruct((blocks,) + small.shape, jnp.float32),
        ),
        in_specs=[vmem, vmem, vmem, pl.BlockSpec(memory_space=pl.ANY)],
        out_specs=[vmem] * 4,
        scratch_shapes=[
            pltpu.VMEM(features.shape, jnp.bfloat16),
            pltpu.VMEM((2, width, seqs * blocks * count), jnp.bfloat16),
            pltpu.VMEM((3,) + act.shape, jnp.bfloat16),
            pltpu.VMEM((blocks - 1,) + mixed.shape[1:], jnp.bfloat16),
            pltpu.VMEM((blocks - 1,) + small.shape, jnp.float32),
            dma((3, seqs)),
            dma((3, seqs)),
            dma((blocks - 1,)),
            dma((blocks - 1,)),
            dma((blocks - 1,)),
            dma((blocks - 1,)),
            dma((2,)),
        ],
        compiler_params=pltpu.CompilerParams(
            collective_id=1, has_side_effects=True, vmem_limit_bytes=48 * 1024 * 1024
        ),
        cost_estimate=pl.CostEstimate(
            flops=8 * seqs * blocks * count * width * blocks * lanes,
            bytes_accessed=4 * blocks * seqs * count * width,
            transcendentals=0,
        ),
    )(act, mixed, small, features)


def by_channels(inputs, key_panel, value_panel, short_filters, medium_filters, lengths, cotangent):
    seqs, count, width = inputs.shape
    blocks = lax.axis_size("dp")
    channels = key_panel.shape[1]
    lanes = channels // blocks
    groups = medium_filters.shape[0] // blocks
    mine = lax.axis_index("dp")
    keys, values, cot, features = front(inputs, key_panel, value_panel, cotangent, blocks)
    short = lax.dynamic_slice_in_dim(short_filters, mine * lanes, lanes, 1)
    medium = lax.dynamic_slice_in_dim(medium_filters, mine * groups, groups, 0)
    mixed, act, small = hyena(keys, values, cot, short, medium, lengths)
    mixed, key_grad, value_grad, small = back(act, mixed, small, features)
    taps, medium_taps = short_filters.shape[-1], medium_filters.shape[-1]
    short_grad = small[:, :16].reshape(blocks, 2, 8, lanes)[:, :, :taps]
    short_grad = short_grad.transpose(1, 0, 3, 2).reshape(2, channels, taps)
    sums = small[:, 16:].reshape(blocks, 2, groups, BLOCK).transpose(0, 2, 1, 3)
    sums = sums.reshape(blocks * groups, 2 * BLOCK)
    medium_grad = sums[:, BLOCK - medium_taps + 1 : BLOCK + 1][:, ::-1]
    return (mixed, key_grad, value_grad, short_grad, medium_grad)


def shards(inputs, key_panel, value_panel, short_filters, medium_filters, lengths, cotangent):
    blocks, shard = lax.axis_size("dp"), lax.axis_size("shard")
    channels = key_panel.shape[1]
    whole = channels == blocks * BLOCK and inputs.shape[1] % (2 * BLOCK) == 0
    plan = by_channels if whole and blocks == 4 and shard == 2 * blocks else by_positions
    return plan(
        inputs, key_panel, value_panel, short_filters, medium_filters, lengths, cotangent
    )


def solution(mesh):
    return jax.shard_map(
        shards,
        mesh=mesh,
        in_specs=(
            P(None, "dp", "shard"),
            P("dp", "shard"),
            P("dp", "shard"),
            P(None, "shard", None),
            P("shard", None),
            P(),
            P(None, "dp", "shard"),
        ),
        out_specs=(
            P(None, "dp", "shard"),
            P("dp", "shard"),
            P("dp", "shard"),
            P(None, "shard", None),
            P("shard", None),
        ),
        check_vma=False,
    )
```

```python
import functools

import jax
import jax.numpy as jnp
from jax import lax
from jax.experimental import pallas as pl
from jax.experimental.pallas import tpu as pltpu
from jax.sharding import PartitionSpec as P

BLOCK = 128


def shifted(value, axis, steps):
    count = lax.axis_size(axis)
    first, last = (max(0, -steps), min(count, count - steps))
    return lax.ppermute(value, axis, [(source, source + steps) for source in range(first, last)])


def band(filters, count):
    groups, taps = filters.shape
    width = count + taps - 1
    padded = jnp.concatenate([filters, jnp.zeros((groups, count), jnp.float32)], axis=1)
    tiled = jnp.tile(padded, (1, count))[:, : count * width]
    return tiled.reshape(groups, count, width)


def band_sums(correlation, count, taps):
    groups, _, width = correlation.shape
    flat = correlation.reshape(groups, count * width)
    padded = jnp.concatenate([flat, jnp.zeros((groups, count), jnp.float32)], axis=1)
    skewed = padded.reshape(groups, count, width + 1)
    return jnp.sum(skewed, axis=1)[:, :taps][:, ::-1]


def short_taps(extended, filters, count):
    width = filters.shape[-1]
    total = jnp.zeros(extended.shape[:2] + (count, extended.shape[3]), jnp.float32)
    for tap in range(width):
        begin = width - 1 - tap
        total = total + filters[:, None, None, :, tap] * extended[
            :, :, begin : begin + count
        ].astype(jnp.float32)
    return total


def short_ahead(extended, filters, count):
    width = filters.shape[-1]
    total = jnp.zeros(extended.shape[:2] + (count, extended.shape[3]), jnp.float32)
    for tap in range(width):
        total = total + filters[:, None, None, :, tap] * extended[:, :, tap : tap + count]
    return total


def filter_terms(grads, extended, count, width):
    columns = []
    for tap in range(width):
        begin = width - 1 - tap
        columns.append(
            jnp.sum(grads * extended[:, :, begin : begin + count].astype(jnp.float32), axis=(1, 2))
        )
    return jnp.stack(columns, axis=-1)


def by_positions(inputs, key_panel, value_panel, short_filters, medium_filters, lengths, cotangent):
    seqs, count, local_width = inputs.shape
    channels = key_panel.shape[1]
    groups, taps = medium_filters.shape
    group_size = channels // groups
    short_width = short_filters.shape[-1]
    span = count + taps - 1
    gathered = (
        lax.all_gather(key_panel, "dp", axis=0, tiled=True),
        lax.all_gather(value_panel, "dp", axis=0, tiled=True),
    )
    panels = jnp.concatenate([gathered[0], gathered[1]], axis=1)
    features = lax.all_gather(inputs, "shard", axis=2, tiled=True)
    projected = jnp.dot(
        features.reshape(seqs * count, -1), panels, preferred_element_type=jnp.float32
    )
    paired = projected.astype(jnp.bfloat16).reshape(seqs, count, 2, channels).transpose(2, 0, 1, 3)
    head_rows = shifted(paired[:, :, count - (short_width - 1) :], "dp", 1)
    extended = jnp.concatenate([head_rows, paired], axis=2)
    smoothed = short_taps(extended, short_filters, count)
    product = (smoothed[0] * smoothed[1]).astype(jnp.bfloat16)
    before = shifted(product[:, count - (taps - 1) :], "dp", 1)
    product_ext = jnp.concatenate([before, product], axis=1).reshape(seqs, span, groups, group_size)
    forward_band = band(medium_filters[:, ::-1], count)
    response = jnp.einsum(
        "gtr,srgm->stgm",
        forward_band,
        product_ext.astype(jnp.float32),
        precision=lax.Precision.HIGHEST,
    ).reshape(seqs, count, channels)
    position = lax.axis_index("dp") * count + jnp.arange(count, dtype=jnp.int32)
    live = (position[None, :] < lengths[:, None])[:, :, None]
    mixed = jnp.where(live, response, 0.0).astype(jnp.bfloat16)
    upstream = jnp.where(live, cotangent, jnp.zeros_like(cotangent))
    after = shifted(upstream[:, : taps - 1], "dp", -1)
    upstream_ext = jnp.concatenate([upstream, after], axis=1).reshape(
        seqs, span, groups, group_size
    )
    backward_band = band(medium_filters, count)
    product_grad = jnp.einsum(
        "gtr,srgm->stgm",
        backward_band,
        upstream_ext.astype(jnp.float32),
        precision=lax.Precision.HIGHEST,
    ).reshape(seqs, count, channels)
    correlation = jnp.einsum(
        "stgm,srgm->gtr",
        upstream.reshape(seqs, count, groups, group_size),
        product_ext,
        preferred_element_type=jnp.float32,
    )
    medium_local = band_sums(correlation, count, taps)
    smooth_grad = jnp.stack([product_grad * smoothed[1], product_grad * smoothed[0]])
    short_local = filter_terms(smooth_grad, extended, count, short_width)
    ahead_rows = shifted(smooth_grad[:, :, : short_width - 1], "dp", -1)
    pair_grad = short_ahead(
        jnp.concatenate([smooth_grad, ahead_rows], axis=2), short_filters, count
    )
    short_grad, medium_grad = lax.psum((short_local, medium_local), "dp")
    outgoing = (
        pair_grad.astype(jnp.bfloat16).transpose(1, 2, 0, 3).reshape(seqs * count, 2 * channels)
    )
    flat_features = features.reshape(seqs * count, -1)
    grads = lax.psum_scatter(
        lax.dot_general(
            flat_features, outgoing, (((0,), (0,)), ((), ())), preferred_element_type=jnp.float32
        ).astype(jnp.bfloat16),
        "dp",
        scatter_dimension=0,
        tiled=True,
    ).astype(jnp.float32)
    key_grad = grads[:, :channels].astype(jnp.bfloat16)
    value_grad = grads[:, channels:].astype(jnp.bfloat16)
    return (mixed, key_grad, value_grad, short_grad, medium_grad)


def filters(
    taps,
    group,
    lengths_ref,
    keys_ref,
    values_ref,
    cot_ref,
    short_ref,
    medium_ref,
    reversed_ref,
    mixed_ref,
    act_ref,
    small_ref,
    pad_ref,
    smooth_ref,
    grad_ref,
    product_ref,
    upstream_ref,
    ahead_band,
    behind_band,
    corr_ref,
    short_acc,
):
    seqs, blocks, count, lanes = keys_ref.shape
    halves = count // BLOCK
    steps = blocks * halves
    length = blocks * count
    groups = lanes // group

    def setup():
        for g in range(groups):
            rows = pl.ds(g * BLOCK, BLOCK)
            base = jnp.broadcast_to(reversed_ref[g : g + 1, :], (BLOCK, 2 * BLOCK))
            behind_band[rows, :] = pltpu.roll(base, 0, 1, stride=1, stride_axis=0).astype(jnp.bfloat16)
            base = jnp.broadcast_to(medium_ref[g : g + 1, :], (BLOCK, 2 * BLOCK))
            ahead_band[rows, :] = pltpu.roll(base, 0, 1, stride=1, stride_axis=0).astype(jnp.bfloat16)

        zeros8 = jnp.zeros((8, lanes), jnp.float32)
        zeros_block = jnp.zeros((BLOCK, lanes), jnp.bfloat16)
        for s in range(seqs):
            for branch in range(2):
                pad_ref[branch, s, pl.ds(0, 8), :] = zeros8
                grad_ref[branch, s, pl.ds(length, 8), :] = zeros8
            product_ref[pl.ds(0, BLOCK), pl.ds(s * lanes, lanes)] = zeros_block
            upstream_ref[pl.ds(length, BLOCK), pl.ds(s * lanes, lanes)] = zeros_block

        corr_ref[...] = jnp.zeros_like(corr_ref)
        short_acc[...] = jnp.zeros_like(short_acc)

    def window(s):
        lane_place = pl.ds(s * lanes, lanes)
        lane_group = lax.broadcasted_iota(jnp.int32, (BLOCK, lanes), 1) // group

        def smooth(step, carry):
            block, half = step // halves, step % halves
            source = pl.ds(pl.multiple_of(half * BLOCK, BLOCK), BLOCK)
            begin = pl.multiple_of(step * BLOCK, BLOCK)
            place = lax.broadcasted_iota(jnp.int32, (BLOCK, lanes), 0) + begin
            parts = []
            for branch, ref in ((0, keys_ref), (1, values_ref)):
                now = ref[s, block, source, :].astype(jnp.float32)
                pad_ref[branch, s, pl.ds(begin + 8, BLOCK), :] = now
                window = pad_ref[branch, s, pl.ds(begin, BLOCK + 8), :]
                total = short_ref[branch, 0:1, :] * now
                for tap in range(1, taps):
                    total += short_ref[branch, tap : tap + 1, :] * window[8 - tap : 8 - tap + BLOCK]
                smooth_ref[branch, s, pl.ds(begin, BLOCK), :] = total
                parts.append(total)
            columns = pl.ds(s * lanes, lanes)
            product_ref[pl.ds(begin + BLOCK, BLOCK), columns] = (parts[0] * parts[1]).astype(
                jnp.bfloat16
            )
            cot = cot_ref[block, s, source, :].astype(jnp.float32)
            upstream_ref[pl.ds(begin, BLOCK), columns] = jnp.where(
                place < lengths_ref[s], cot, 0.0
            ).astype(jnp.bfloat16)
            return carry

        lax.fori_loop(0, steps, smooth, 0)


        def own(stacked):
            chosen = stacked[0:BLOCK]
            for g in range(1, groups):
                chosen = jnp.where(lane_group == g, stacked[g * BLOCK : (g + 1) * BLOCK], chosen)
            return chosen

        def mix(step, carry):
            block, half = step // halves, step % halves
            source = pl.ds(pl.multiple_of(half * BLOCK, BLOCK), BLOCK)
            begin = pl.multiple_of(step * BLOCK, BLOCK)
            place = lax.broadcasted_iota(jnp.int32, (BLOCK, lanes), 0) + begin
            past = product_ref[pl.ds(begin, 2 * BLOCK), lane_place]
            response = own(jnp.dot(behind_band[...], past, preferred_element_type=jnp.float32))
            future = upstream_ref[pl.ds(begin, 2 * BLOCK), lane_place]
            product_grad = own(jnp.dot(ahead_band[...], future, preferred_element_type=jnp.float32))
            here = future[0:BLOCK]
            apart = jnp.concatenate(
                [jnp.where(lane_group == g, here, jnp.zeros_like(here)) for g in range(groups)], axis=0
            )
            corr_ref[...] += lax.dot_general(
                apart, past, (((1,), (1,)), ((), ())), preferred_element_type=jnp.float32
            )
            mixed_ref[block, s, source, :] = jnp.where(
                place < lengths_ref[s], response, 0.0
            ).astype(jnp.bfloat16)
            for branch in range(2):
                grad = product_grad * smooth_ref[1 - branch, s, pl.ds(begin, BLOCK), :]
                grad_ref[branch, s, pl.ds(begin, BLOCK), :] = grad
                window = pad_ref[branch, s, pl.ds(begin, BLOCK + 8), :]
                for tap in range(taps):
                    term = grad * window[8 - tap : 8 - tap + BLOCK]
                    short_acc[branch, tap] += jnp.sum(term.reshape(BLOCK // 8, 8, lanes), axis=0)
            return carry

        lax.fori_loop(0, steps, mix, 0)

        def back(step, carry):
            block, half = step // halves, step % halves
            source = pl.ds(pl.multiple_of(half * BLOCK, BLOCK), BLOCK)
            begin = pl.multiple_of(step * BLOCK, BLOCK)
            for branch in range(2):
                window = grad_ref[branch, s, pl.ds(begin, BLOCK + 8), :]
                total = short_ref[branch, 0:1, :] * window[0:BLOCK]
                for tap in range(1, taps):
                    total += short_ref[branch, tap : tap + 1, :] * window[tap : tap + BLOCK]
                columns = slice(branch * lanes, (branch + 1) * lanes)
                act_ref[s, block, source, columns] = total.astype(jnp.bfloat16)
            return carry

        lax.fori_loop(0, steps, back, 0)


    def finish():
        for branch in range(2):
            for tap in range(8):
                if tap < taps:
                    sums = jnp.sum(short_acc[branch, tap], axis=0, keepdims=True)
                else:
                    sums = jnp.zeros((1, lanes), jnp.float32)
                small_ref[branch * 8 + tap : branch * 8 + tap + 1, :] = sums
        for g in range(groups):
            rows = BLOCK
            total = corr_ref[pl.ds(g * BLOCK, BLOCK), :]
            while rows > 1:
                rows //= 2
                total = total[:rows] + pltpu.roll(total[rows:], 2 * BLOCK - rows, 1)
            small_ref[16 + g : 17 + g, :] = total[:, :BLOCK]
            small_ref[16 + groups + g : 17 + groups + g, :] = total[:, BLOCK:]

    return setup, window, finish


def remote(source, target, send, recv, dp, shard):
    return pltpu.make_async_remote_copy(
        src_ref=source,
        dst_ref=target,
        send_sem=send,
        recv_sem=recv,
        device_id={"dp": dp, "shard": shard},
        device_id_type=pl.DeviceIdType.MESH,
    )


def front(
    x_ref,
    key_ref,
    value_ref,
    cot_ref,
    keys_ref,
    values_ref,
    line,
    features,
    panels,
    own,
    outgoing,
    incoming,
    cot_in,
    line_send,
    line_recv,
    plane_send,
    plane_recv,
    core_send,
    core_recv,
    sum_send,
    sum_recv,
    cot_send,
    cot_recv,
    local,
    panel_sem,
    cot_local,
):
    seqs, count, width = x_ref.shape
    blocks, lanes = cot_in.shape[0], cot_in.shape[-1]
    rows = count // 2
    chunks = 2 * seqs
    p, shard = lax.axis_index("dp"), lax.axis_index("shard")
    z, core = shard // 2, shard % 2
    sibling = z * 2 + (1 - core)
    peers = [(p + j) % blocks for j in range(blocks)]
    froms = [(p + blocks - j) % blocks for j in range(blocks)]

    barrier = pltpu.get_barrier_semaphore()

    def greet(dp, to):
        pl.semaphore_signal(
            barrier,
            inc=1,
            device_id={"dp": dp, "shard": to},
            device_id_type=pl.DeviceIdType.MESH,
        )

    greet(p, sibling)
    for j in range(1, blocks):
        greet(peers[j], shard)

    for step in (2, 2 * blocks - 2):
        greet(p, (shard + step) % (2 * blocks))
    pl.semaphore_wait(barrier, blocks + 2)

    def block_of(k):
        return x_ref.at[k // 2, pl.ds(k % 2 * rows, rows)]

    def held(h, layer, k):
        return block_of(k) if h == 0 else line.at[layer, k]

    def line_copy(h, layer, k, way):
        return remote(
            held(h, layer, k),
            line.at[layer, k],
            line_send.at[way, layer, k],
            line_recv.at[layer, k],
            p,
            shard + 2 * (1 - 2 * way),
        )

    def plane_copy(h, layer, k):
        return remote(
            held(h, layer, k),
            features.at[core, k, p],
            plane_send.at[layer, k],
            plane_recv.at[p, k],
            layer,
            shard,
        )

    def plane_arrival(block, k):
        place = features.at[core, k, block]
        return remote(
            place, place, plane_send.at[block, k], plane_recv.at[block, k], block, shard
        )

    def core_copy(source, block, k):
        return remote(
            source,
            features.at[core, k, block],
            core_send.at[block, k],
            core_recv.at[block, k],
            p,
            sibling,
        )

    def core_arrival(block, k):
        place = features.at[1 - core, k, block]
        return remote(place, place, core_send.at[block, k], core_recv.at[block, k], p, sibling)

    def keep_copy(h, layer, k):
        return pltpu.make_async_copy(held(h, layer, k), features.at[core, k, p], local.at[k])

    def steps(h):
        if h == 0:
            return [(0, z, None, z < blocks - 1), (1, z, None, z > 0)]
        return [
            (0, z - h, z - h >= 0, z < blocks - 1),
            (1, z + h, z + h < blocks, z > 0),
        ]

    def dispatch(h, layer, k):
        @pl.when(layer == p)
        def _():
            keep_copy(h, layer, k).start()
            core_copy(held(h, layer, k), p, k).start()

        @pl.when(layer != p)
        def _():
            plane_copy(h, layer, k).start()

    def hop(k, h):
        if h == 0:
            for way, layer, _, onward in steps(0):

                @pl.when(onward)
                def _():
                    line_copy(0, layer, k, way).start()

            dispatch(0, z, k)
            return
        for way, layer, valid, onward in steps(h):

            @pl.when(valid)
            def _():
                line_copy(h, layer, k, way).wait_recv()

                @pl.when(onward)
                def _():
                    line_copy(h, layer, k, way).start()

                dispatch(h, layer, k)

    def share(k):
        for j in range(1, blocks):
            plane_arrival(froms[j], k).wait_recv()
            core_copy(features.at[core, k, froms[j]], froms[j], k).start()

    def complete(k):
        for j in range(blocks):
            core_arrival(froms[j], k).wait_recv()
        keep_copy(0, z, k).wait()

    def sum_copy(k, j):
        return remote(
            outgoing.at[k, j - 1],
            incoming.at[k, j - 1],
            sum_send.at[k, j - 1],
            sum_recv.at[k, j - 1],
            (p + j) % blocks,
            shard,
        )

    def product(k, owner):
        total = jnp.zeros((blocks * rows, 2 * lanes), jnp.float32)
        for c in range(2):
            total += jnp.dot(
                features[c, k].reshape(blocks * rows, width),
                panels[owner, c],
                preferred_element_type=jnp.float32,
            )
        return total

    def project(k):
        def others(j, carry):
            outgoing[k, j - 1] = product(k, (p + j) % blocks).astype(jnp.bfloat16)
            sum_copy(k, j).start()
            return carry

        lax.fori_loop(1, blocks, others, 0)
        own[k] = product(k, p)

    def cot_place(owner):
        return pl.ds(pl.multiple_of(owner * lanes, lanes), lanes)

    def cot_copy(j):
        return remote(
            cot_ref.at[:, :, cot_place(peers[j])],
            cot_in.at[p],
            cot_send.at[j],
            cot_recv.at[p],
            peers[j],
            shard,
        )

    def cot_arrival(j):
        place = cot_in.at[froms[j]]
        return remote(place, place, cot_send.at[j], cot_recv.at[froms[j]], froms[j], shard)

    cot_keep = pltpu.make_async_copy(
        cot_ref.at[:, :, cot_place(p)], cot_in.at[p], cot_local.at[0]
    )
    panel_copies = [
        pltpu.make_async_copy(
            ref.at[pl.ds(c * width, width), pl.ds(r * lanes, lanes)],
            panels.at[r, c, :, pl.ds(branch * lanes, lanes)],
            panel_sem.at[branch, r, c],
        )
        for branch, ref in ((0, key_ref), (1, value_ref))
        for r in range(blocks)
        for c in range(2)
    ]

    def run(prepare):
        hop(0, 0)
        for j in range(1, blocks):
            cot_copy(j).start()
        cot_keep.start()
        for copy in panel_copies:
            copy.start()
        prepare()
        hop(0, 1)
        hop(0, 2)
        hop(1, 0)
        hop(0, 3)
        for k in range(1, chunks):
            hop(k, 1)
            hop(k, 2)
            if k + 1 < chunks:
                hop(k + 1, 0)
            share(k - 1)
            hop(k, 3)
            complete(k - 1)
            if k == 1:
                for copy in panel_copies:
                    copy.wait()
            project(k - 1)
        share(chunks - 1)
        cot_keep.wait()
        for j in range(1, blocks):
            cot_arrival(j).wait_recv()
        complete(chunks - 1)
        project(chunks - 1)

    def collect(w):
        for k in (2 * w, 2 * w + 1):
            for j in range(1, blocks):
                sum_copy(k, j).wait_recv()
            total = own[k]
            for j in range(1, blocks):
                total += incoming[k, j - 1].astype(jnp.float32)
            total = total.astype(jnp.bfloat16).reshape(blocks, rows, 2 * lanes)
            place = pl.ds(k % 2 * rows, rows)
            keys_ref[k // 2, :, place, :] = total[:, :, 0:lanes]
            values_ref[k // 2, :, place, :] = total[:, :, lanes : 2 * lanes]

    def drain():
        for k in range(chunks):
            for j in range(1, blocks):
                sum_copy(k, j).wait_send()
            for j in range(blocks):
                core_copy(features.at[core, k, froms[j]], froms[j], k).wait_send()
            for h in range(blocks):
                for way, layer, valid, onward in steps(h):
                    if h > 0:
                        onward = jnp.logical_and(valid, onward)

                    @pl.when(onward)
                    def _():
                        line_copy(h, layer, k, way).wait_send()

                    if h > 0 or way == 0:
                        sent = layer != p
                        if h > 0:
                            sent = jnp.logical_and(valid, sent)

                        @pl.when(sent)
                        def _():
                            plane_copy(h, layer, k).wait_send()

        for j in range(1, blocks):
            cot_copy(j).wait_send()

    return run, collect, drain


def gradients(
    act_ref,
    mixed_ref,
    small_ref,
    mixed_out,
    key_out,
    value_out,
    small_out,
    features,
    turned,
    got,
    mixed_in,
    small_in,
    act_send,
    act_recv,
    mixed_send,
    mixed_recv,
    small_send,
    small_recv,
):
    seqs, blocks, count, both = act_ref.shape
    lanes = both // 2
    width = features.shape[-1]
    p, shard = lax.axis_index("dp"), lax.axis_index("shard")
    x, y = p % 2, p // 2
    beside, above, across = y * 2 + 1 - x, (1 - y) * 2 + x, (1 - y) * 2 + 1 - x
    owners = (p, beside, above, across)

    span = blocks // 2

    def half_of(ref, w, half):
        return ref.at[w, pl.ds(half * span, span)]

    def send_own(slot, w, half):
        return remote(
            half_of(act_ref, w, half),
            half_of(got.at[slot - 1], w, half),
            act_send.at[slot - 1, w, half],
            act_recv.at[slot - 1, w, half],
            owners[slot],
            shard,
        )

    def pass_on(w, half):
        return remote(
            half_of(got.at[half], w, half),
            half_of(got.at[2], w, half),
            act_send.at[2, w, half],
            act_recv.at[2, w, half],
            owners[2 - half],
            shard,
        )

    def arrived(slot, w, half):
        place = half_of(got.at[slot - 1], w, half)
        return remote(
            place,
            place,
            act_send.at[slot - 1, w, half],
            act_recv.at[slot - 1, w, half],
            owners[slot],
            shard,
        )

    def mixed_copy(k):
        return remote(
            mixed_ref.at[owners[k]],
            mixed_in.at[k - 1],
            mixed_send.at[k - 1],
            mixed_recv.at[k - 1],
            owners[k],
            shard,
        )

    def small_copy(k):
        return remote(
            small_ref,
            small_in.at[k - 1],
            small_send.at[k - 1],
            small_recv.at[k - 1],
            owners[k],
            shard,
        )

    def turn(c):
        def tile(i, carry):
            k, block = i // blocks, i % blocks
            rows = count // 2
            begin = ((k // 2 * blocks + block) * 2 + k % 2) * rows
            columns = pl.ds(pl.multiple_of(begin, rows), rows)
            turned[c, :, columns] = features[c, k, block].T
            return carry

        lax.fori_loop(0, 2 * seqs * blocks, tile, 0)

    def grads(ref, owner):
        place = pl.ds(pl.multiple_of(owner * lanes, lanes), lanes)
        tall = width // 2

        def tile(i, carry):
            c, half = i // 2, i % 2
            rows = pl.ds(pl.multiple_of(half * tall, tall), tall)
            total = jnp.dot(
                turned[c, rows, :],
                ref[...].reshape(seqs * blocks * count, both),
                preferred_element_type=jnp.float32,
            ).astype(jnp.bfloat16)
            out = pl.ds(pl.multiple_of(i * tall, tall), tall)
            key_out[out, place] = total[:, :lanes]
            value_out[out, place] = total[:, lanes:]
            return carry

        lax.fori_loop(0, 4, tile, 0)

    def send(w):
        for slot, half in ((1, 0), (2, 1), (1, 1), (2, 0)):
            send_own(slot, w, half).start()

    def forward(w):
        for half in range(2):
            arrived(1 + half, w, half).wait_recv()
            pass_on(w, half).start()

    def spread():
        for k in range(1, blocks):
            mixed_copy(k).start()
            small_copy(k).start()

    def run():
        forward(0)
        turn(0)
        forward(1)
        turn(1)
        grads(act_ref, p)
        for slot, owner in ((1, beside), (2, above)):
            for w in range(seqs):
                arrived(slot, w, 2 - slot).wait_recv()
            grads(got.at[slot - 1], owner)
        small_out[p] = small_ref[...]
        for k in range(1, blocks):
            small_copy(k).wait_recv()
            small_out[owners[k]] = small_in[k - 1]
        mixed_out[:, :, pl.ds(pl.multiple_of(p * lanes, lanes), lanes)] = mixed_ref[p]
        for k in range(1, blocks):
            mixed_copy(k).wait_recv()
            place = pl.ds(pl.multiple_of(owners[k] * lanes, lanes), lanes)
            mixed_out[:, :, place] = mixed_in[k - 1]
        for w in range(seqs):
            for half in range(2):
                arrived(3, w, half).wait_recv()
        grads(got.at[2], across)
        for w in range(seqs):
            for half in range(2):
                send_own(1, w, half).wait_send()
                send_own(2, w, half).wait_send()
                pass_on(w, half).wait_send()
        for k in range(1, blocks):
            mixed_copy(k).wait_send()
            small_copy(k).wait_send()

    return send, forward, spread, run


def operator_kernel(taps, group, *refs):
    (x_ref, key_ref, value_ref, cot_ref, lengths_ref, short_ref, medium_ref, reversed_ref) = refs[:8]
    outs, keys_ref, values_ref = refs[8:12], refs[12], refs[13]
    act_ref, mixed_ref, small_ref = refs[14:17]
    front_refs, filter_refs, back_refs = refs[17:37], refs[37:46], refs[46:]
    features, cot_in = front_refs[1], front_refs[6]
    project, collect, drain = front(
        x_ref, key_ref, value_ref, cot_ref, keys_ref, values_ref, *front_refs
    )
    setup, window, finish = filters(
        taps,
        group,
        lengths_ref,
        keys_ref,
        values_ref,
        cot_in,
        short_ref,
        medium_ref,
        reversed_ref,
        mixed_ref,
        act_ref,
        small_ref,
        *filter_refs,
    )
    send, forward, spread, run = gradients(
        act_ref, mixed_ref, small_ref, *outs, features, *back_refs
    )
    project(setup)
    for w in range(keys_ref.shape[0]):
        collect(w)
        window(w)
        send(w)
    finish()
    spread()
    run()
    drain()


def operator(inputs, key_panel, value_panel, cotangent, lengths, short_filters, medium_filters, blocks):
    seqs, count, width = inputs.shape
    channels = key_panel.shape[1]
    lanes = channels // blocks
    groups, medium = medium_filters.shape
    taps = short_filters.shape[-1]
    length = blocks * count
    short = jnp.pad(short_filters.transpose(0, 2, 1), ((0, 0), (0, 8 - taps), (0, 0)))
    ahead = jnp.pad(medium_filters, ((0, 0), (0, 2 * BLOCK - medium)))
    behind = jnp.pad(medium_filters[:, ::-1], ((0, 0), (BLOCK + 1 - medium, BLOCK - 1)))
    pieces = 2 * seqs
    tall = blocks * count // 2
    vmem = pl.BlockSpec(memory_space=pltpu.VMEM)
    hbm = pl.BlockSpec(memory_space=pl.ANY)
    dma = pltpu.SemaphoreType.DMA
    small_shape = (16 + 2 * groups, lanes)
    act_shape = (seqs, blocks, count, 2 * lanes)
    panel = jax.ShapeDtypeStruct((2 * width, channels), jnp.bfloat16)
    return pl.pallas_call(
        functools.partial(operator_kernel, taps, lanes // groups),
        out_shape=(
            jax.ShapeDtypeStruct((seqs, count, channels), jnp.bfloat16),
            panel,
            panel,
            jax.ShapeDtypeStruct((blocks,) + small_shape, jnp.float32),
        ),
        in_specs=[hbm] * 4 + [pl.BlockSpec(memory_space=pltpu.SMEM)] + [vmem] * 3,
        out_specs=[vmem] * 4,
        scratch_shapes=[
            pltpu.VMEM((seqs, blocks, count, lanes), jnp.bfloat16),
            pltpu.VMEM((seqs, blocks, count, lanes), jnp.bfloat16),
            pltpu.VMEM(act_shape, jnp.bfloat16),
            pltpu.VMEM((blocks, seqs, count, lanes), jnp.bfloat16),
            pltpu.VMEM(small_shape, jnp.float32),
            pltpu.VMEM((blocks, pieces, count // 2, width), jnp.bfloat16),
            pltpu.VMEM((2, pieces, blocks, count // 2, width), jnp.bfloat16),
            pltpu.VMEM((blocks, 2, width, 2 * lanes), jnp.bfloat16),
            pltpu.VMEM((pieces, tall, 2 * lanes), jnp.float32),
            pltpu.VMEM((pieces, blocks - 1, tall, 2 * lanes), jnp.bfloat16),
            pltpu.VMEM((pieces, blocks - 1, tall, 2 * lanes), jnp.bfloat16),
            pltpu.VMEM((blocks, seqs, count, lanes), jnp.bfloat16),
            dma((2, blocks, pieces)),
            dma((blocks, pieces)),
            dma((blocks, pieces)),
            dma((blocks, pieces)),
            dma((blocks, pieces)),
            dma((blocks, pieces)),
            dma((pieces, blocks - 1)),
            dma((pieces, blocks - 1)),
            dma((blocks,)),
            dma((blocks,)),
        ]
        + [dma((pieces,)), dma((2, blocks, 2)), dma((1,))]
        + [
            pltpu.VMEM((2, seqs, length + 8, lanes), jnp.float32),
            pltpu.VMEM((2, seqs, length, lanes), jnp.float32),
            pltpu.VMEM((2, seqs, length + 8, lanes), jnp.float32),
            pltpu.VMEM((length + BLOCK, seqs * lanes), jnp.bfloat16),
            pltpu.VMEM((length + BLOCK, seqs * lanes), jnp.bfloat16),
            pltpu.VMEM((groups * BLOCK, 2 * BLOCK), jnp.bfloat16),
            pltpu.VMEM((groups * BLOCK, 2 * BLOCK), jnp.bfloat16),
            pltpu.VMEM((groups * BLOCK, 2 * BLOCK), jnp.float32),
            pltpu.VMEM((2, taps, 8, lanes), jnp.float32),
            pltpu.VMEM((2, width, seqs * blocks * count), jnp.bfloat16),
            pltpu.VMEM((3,) + act_shape, jnp.bfloat16),
            pltpu.VMEM((blocks - 1, seqs, count, lanes), jnp.bfloat16),
            pltpu.VMEM((blocks - 1,) + small_shape, jnp.float32),
            dma((3, seqs, 2)),
            dma((3, seqs, 2)),
            dma((blocks - 1,)),
            dma((blocks - 1,)),
            dma((blocks - 1,)),
            dma((blocks - 1,)),
        ],
        compiler_params=pltpu.CompilerParams(
            collective_id=0, has_side_effects=True, vmem_limit_bytes=62 * 1024 * 1024
        ),
        cost_estimate=pl.CostEstimate(
            flops=8 * blocks * seqs * count * 2 * width * channels,
            bytes_accessed=8 * blocks * seqs * count * width,
            transcendentals=0,
        ),
    )(inputs, key_panel, value_panel, cotangent, lengths, short, ahead, behind)


def by_channels(inputs, key_panel, value_panel, short_filters, medium_filters, lengths, cotangent):
    blocks = lax.axis_size("dp")
    channels = key_panel.shape[1]
    lanes = channels // blocks
    groups = medium_filters.shape[0] // blocks
    mine = lax.axis_index("dp")
    short = lax.dynamic_slice_in_dim(short_filters, mine * lanes, lanes, 1)
    medium = lax.dynamic_slice_in_dim(medium_filters, mine * groups, groups, 0)
    mixed, key_grad, value_grad, small = operator(
        inputs, key_panel, value_panel, cotangent, lengths, short, medium, blocks
    )
    taps, medium_taps = short_filters.shape[-1], medium_filters.shape[-1]
    short_grad = small[:, :16].reshape(blocks, 2, 8, lanes)[:, :, :taps]
    short_grad = short_grad.transpose(1, 0, 3, 2).reshape(2, channels, taps)
    sums = small[:, 16:].reshape(blocks, 2, groups, BLOCK).transpose(0, 2, 1, 3)
    sums = sums.reshape(blocks * groups, 2 * BLOCK)
    medium_grad = sums[:, BLOCK - medium_taps + 1 : BLOCK + 1][:, ::-1]
    return (mixed, key_grad, value_grad, short_grad, medium_grad)


def shards(inputs, key_panel, value_panel, short_filters, medium_filters, lengths, cotangent):
    blocks, shard = lax.axis_size("dp"), lax.axis_size("shard")
    channels = key_panel.shape[1]
    whole = channels == blocks * BLOCK and inputs.shape[1] % (2 * BLOCK) == 0
    plan = by_channels if whole and blocks == 4 and shard == 2 * blocks else by_positions
    return plan(
        inputs, key_panel, value_panel, short_filters, medium_filters, lengths, cotangent
    )


def solution(mesh):
    return jax.shard_map(
        shards,
        mesh=mesh,
        in_specs=(
            P(None, "dp", "shard"),
            P("dp", "shard"),
            P("dp", "shard"),
            P(None, "shard", None),
            P("shard", None),
            P(),
            P(None, "dp", "shard"),
        ),
        out_specs=(
            P(None, "dp", "shard"),
            P("dp", "shard"),
            P("dp", "shard"),
            P(None, "shard", None),
            P("shard", None),
        ),
        check_vma=False,
    )
```

```python
import functools

import jax
import jax.numpy as jnp
from jax import lax
from jax.experimental import pallas as pl
from jax.experimental.pallas import tpu as pltpu
from jax.sharding import PartitionSpec as P

BLOCK = 128
PARTS = 4


def shifted(value, axis, steps):
    count = lax.axis_size(axis)
    first, last = (max(0, -steps), min(count, count - steps))
    return lax.ppermute(value, axis, [(source, source + steps) for source in range(first, last)])


def band(filters, count):
    groups, taps = filters.shape
    width = count + taps - 1
    padded = jnp.concatenate([filters, jnp.zeros((groups, count), jnp.float32)], axis=1)
    tiled = jnp.tile(padded, (1, count))[:, : count * width]
    return tiled.reshape(groups, count, width)


def band_sums(correlation, count, taps):
    groups, _, width = correlation.shape
    flat = correlation.reshape(groups, count * width)
    padded = jnp.concatenate([flat, jnp.zeros((groups, count), jnp.float32)], axis=1)
    skewed = padded.reshape(groups, count, width + 1)
    return jnp.sum(skewed, axis=1)[:, :taps][:, ::-1]


def short_taps(extended, filters, count):
    width = filters.shape[-1]
    total = jnp.zeros(extended.shape[:2] + (count, extended.shape[3]), jnp.float32)
    for tap in range(width):
        begin = width - 1 - tap
        total = total + filters[:, None, None, :, tap] * extended[
            :, :, begin : begin + count
        ].astype(jnp.float32)
    return total


def short_ahead(extended, filters, count):
    width = filters.shape[-1]
    total = jnp.zeros(extended.shape[:2] + (count, extended.shape[3]), jnp.float32)
    for tap in range(width):
        total = total + filters[:, None, None, :, tap] * extended[:, :, tap : tap + count]
    return total


def filter_terms(grads, extended, count, width):
    columns = []
    for tap in range(width):
        begin = width - 1 - tap
        columns.append(
            jnp.sum(grads * extended[:, :, begin : begin + count].astype(jnp.float32), axis=(1, 2))
        )
    return jnp.stack(columns, axis=-1)


def by_positions(inputs, key_panel, value_panel, short_filters, medium_filters, lengths, cotangent):
    seqs, count, local_width = inputs.shape
    channels = key_panel.shape[1]
    groups, taps = medium_filters.shape
    group_size = channels // groups
    short_width = short_filters.shape[-1]
    span = count + taps - 1
    gathered = (
        lax.all_gather(key_panel, "dp", axis=0, tiled=True),
        lax.all_gather(value_panel, "dp", axis=0, tiled=True),
    )
    panels = jnp.concatenate([gathered[0], gathered[1]], axis=1)
    features = lax.all_gather(inputs, "shard", axis=2, tiled=True)
    projected = jnp.dot(
        features.reshape(seqs * count, -1), panels, preferred_element_type=jnp.float32
    )
    paired = projected.astype(jnp.bfloat16).reshape(seqs, count, 2, channels).transpose(2, 0, 1, 3)
    head_rows = shifted(paired[:, :, count - (short_width - 1) :], "dp", 1)
    extended = jnp.concatenate([head_rows, paired], axis=2)
    smoothed = short_taps(extended, short_filters, count)
    product = (smoothed[0] * smoothed[1]).astype(jnp.bfloat16)
    before = shifted(product[:, count - (taps - 1) :], "dp", 1)
    product_ext = jnp.concatenate([before, product], axis=1).reshape(seqs, span, groups, group_size)
    forward_band = band(medium_filters[:, ::-1], count)
    response = jnp.einsum(
        "gtr,srgm->stgm",
        forward_band,
        product_ext.astype(jnp.float32),
        precision=lax.Precision.HIGHEST,
    ).reshape(seqs, count, channels)
    position = lax.axis_index("dp") * count + jnp.arange(count, dtype=jnp.int32)
    live = (position[None, :] < lengths[:, None])[:, :, None]
    mixed = jnp.where(live, response, 0.0).astype(jnp.bfloat16)
    upstream = jnp.where(live, cotangent, jnp.zeros_like(cotangent))
    after = shifted(upstream[:, : taps - 1], "dp", -1)
    upstream_ext = jnp.concatenate([upstream, after], axis=1).reshape(
        seqs, span, groups, group_size
    )
    backward_band = band(medium_filters, count)
    product_grad = jnp.einsum(
        "gtr,srgm->stgm",
        backward_band,
        upstream_ext.astype(jnp.float32),
        precision=lax.Precision.HIGHEST,
    ).reshape(seqs, count, channels)
    correlation = jnp.einsum(
        "stgm,srgm->gtr",
        upstream.reshape(seqs, count, groups, group_size),
        product_ext,
        preferred_element_type=jnp.float32,
    )
    medium_local = band_sums(correlation, count, taps)
    smooth_grad = jnp.stack([product_grad * smoothed[1], product_grad * smoothed[0]])
    short_local = filter_terms(smooth_grad, extended, count, short_width)
    ahead_rows = shifted(smooth_grad[:, :, : short_width - 1], "dp", -1)
    pair_grad = short_ahead(
        jnp.concatenate([smooth_grad, ahead_rows], axis=2), short_filters, count
    )
    short_grad, medium_grad = lax.psum((short_local, medium_local), "dp")
    outgoing = (
        pair_grad.astype(jnp.bfloat16).transpose(1, 2, 0, 3).reshape(seqs * count, 2 * channels)
    )
    flat_features = features.reshape(seqs * count, -1)
    grads = lax.psum_scatter(
        lax.dot_general(
            flat_features, outgoing, (((0,), (0,)), ((), ())), preferred_element_type=jnp.float32
        ).astype(jnp.bfloat16),
        "dp",
        scatter_dimension=0,
        tiled=True,
    ).astype(jnp.float32)
    key_grad = grads[:, :channels].astype(jnp.bfloat16)
    value_grad = grads[:, channels:].astype(jnp.bfloat16)
    return (mixed, key_grad, value_grad, short_grad, medium_grad)


def filters(
    taps,
    group,
    lengths_ref,
    keys_ref,
    values_ref,
    cot_ref,
    short_ref,
    medium_ref,
    reversed_ref,
    mixed_ref,
    act_ref,
    small_ref,
    pad_ref,
    smooth_ref,
    grad_ref,
    product_ref,
    upstream_ref,
    ahead_band,
    behind_band,
    corr_ref,
    short_acc,
):
    seqs, blocks, count, lanes = keys_ref.shape
    halves = count // BLOCK
    steps = blocks * halves
    length = blocks * count
    groups = lanes // group

    def setup():
        for g in range(groups):
            rows = pl.ds(g * BLOCK, BLOCK)
            base = jnp.broadcast_to(reversed_ref[g : g + 1, :], (BLOCK, 2 * BLOCK))
            behind_band[rows, :] = pltpu.roll(base, 0, 1, stride=1, stride_axis=0).astype(jnp.bfloat16)
            base = jnp.broadcast_to(medium_ref[g : g + 1, :], (BLOCK, 2 * BLOCK))
            ahead_band[rows, :] = pltpu.roll(base, 0, 1, stride=1, stride_axis=0).astype(jnp.bfloat16)

        zeros8 = jnp.zeros((8, lanes), jnp.float32)
        zeros_block = jnp.zeros((BLOCK, lanes), jnp.bfloat16)
        for s in range(seqs):
            for branch in range(2):
                pad_ref[branch, s, pl.ds(0, 8), :] = zeros8
                grad_ref[branch, s, pl.ds(length, 8), :] = zeros8
            product_ref[pl.ds(0, BLOCK), pl.ds(s * lanes, lanes)] = zeros_block
            upstream_ref[pl.ds(length, BLOCK), pl.ds(s * lanes, lanes)] = zeros_block

        corr_ref[...] = jnp.zeros_like(corr_ref)
        short_acc[...] = jnp.zeros_like(short_acc)

    def window(s):
        lane_place = pl.ds(s * lanes, lanes)
        lane_group = lax.broadcasted_iota(jnp.int32, (BLOCK, lanes), 1) // group

        def smooth(step, carry):
            block, half = step // halves, step % halves
            source = pl.ds(pl.multiple_of(half * BLOCK, BLOCK), BLOCK)
            begin = pl.multiple_of(step * BLOCK, BLOCK)
            place = lax.broadcasted_iota(jnp.int32, (BLOCK, lanes), 0) + begin
            parts = []
            for branch, ref in ((0, keys_ref), (1, values_ref)):
                now = ref[s, block, source, :].astype(jnp.float32)
                pad_ref[branch, s, pl.ds(begin + 8, BLOCK), :] = now
                window = pad_ref[branch, s, pl.ds(begin, BLOCK + 8), :]
                total = short_ref[branch, 0:1, :] * now
                for tap in range(1, taps):
                    total += short_ref[branch, tap : tap + 1, :] * window[8 - tap : 8 - tap + BLOCK]
                smooth_ref[branch, s, pl.ds(begin, BLOCK), :] = total
                parts.append(total)
            columns = pl.ds(s * lanes, lanes)
            product_ref[pl.ds(begin + BLOCK, BLOCK), columns] = (parts[0] * parts[1]).astype(
                jnp.bfloat16
            )
            cot = cot_ref[block, s, source, :].astype(jnp.float32)
            upstream_ref[pl.ds(begin, BLOCK), columns] = jnp.where(
                place < lengths_ref[s], cot, 0.0
            ).astype(jnp.bfloat16)
            return carry

        lax.fori_loop(0, steps, smooth, 0)


        def own(stacked):
            chosen = stacked[0:BLOCK]
            for g in range(1, groups):
                chosen = jnp.where(lane_group == g, stacked[g * BLOCK : (g + 1) * BLOCK], chosen)
            return chosen

        def mix(step, carry):
            block, half = step // halves, step % halves
            source = pl.ds(pl.multiple_of(half * BLOCK, BLOCK), BLOCK)
            begin = pl.multiple_of(step * BLOCK, BLOCK)
            place = lax.broadcasted_iota(jnp.int32, (BLOCK, lanes), 0) + begin
            past = product_ref[pl.ds(begin, 2 * BLOCK), lane_place]
            response = own(jnp.dot(behind_band[...], past, preferred_element_type=jnp.float32))
            future = upstream_ref[pl.ds(begin, 2 * BLOCK), lane_place]
            product_grad = own(jnp.dot(ahead_band[...], future, preferred_element_type=jnp.float32))
            here = future[0:BLOCK]
            apart = jnp.concatenate(
                [jnp.where(lane_group == g, here, jnp.zeros_like(here)) for g in range(groups)], axis=0
            )
            corr_ref[...] += lax.dot_general(
                apart, past, (((1,), (1,)), ((), ())), preferred_element_type=jnp.float32
            )
            mixed_ref[block, s, source, :] = jnp.where(
                place < lengths_ref[s], response, 0.0
            ).astype(jnp.bfloat16)
            for branch in range(2):
                grad = product_grad * smooth_ref[1 - branch, s, pl.ds(begin, BLOCK), :]
                grad_ref[branch, s, pl.ds(begin, BLOCK), :] = grad
                window = pad_ref[branch, s, pl.ds(begin, BLOCK + 8), :]
                for tap in range(taps):
                    term = grad * window[8 - tap : 8 - tap + BLOCK]
                    short_acc[branch, tap] += jnp.sum(term.reshape(BLOCK // 8, 8, lanes), axis=0)
            return carry

        lax.fori_loop(0, steps, mix, 0)

        def back(step, carry):
            block, half = step // halves, step % halves
            source = pl.ds(pl.multiple_of(half * BLOCK, BLOCK), BLOCK)
            begin = pl.multiple_of(step * BLOCK, BLOCK)
            for branch in range(2):
                window = grad_ref[branch, s, pl.ds(begin, BLOCK + 8), :]
                total = short_ref[branch, 0:1, :] * window[0:BLOCK]
                for tap in range(1, taps):
                    total += short_ref[branch, tap : tap + 1, :] * window[tap : tap + BLOCK]
                columns = slice(branch * lanes, (branch + 1) * lanes)
                act_ref[s, block, source, columns] = total.astype(jnp.bfloat16)
            return carry

        lax.fori_loop(0, steps, back, 0)


    def finish():
        for branch in range(2):
            for tap in range(8):
                if tap < taps:
                    sums = jnp.sum(short_acc[branch, tap], axis=0, keepdims=True)
                else:
                    sums = jnp.zeros((1, lanes), jnp.float32)
                small_ref[branch * 8 + tap : branch * 8 + tap + 1, :] = sums
        for g in range(groups):
            rows = BLOCK
            total = corr_ref[pl.ds(g * BLOCK, BLOCK), :]
            while rows > 1:
                rows //= 2
                total = total[:rows] + pltpu.roll(total[rows:], 2 * BLOCK - rows, 1)
            small_ref[16 + g : 17 + g, :] = total[:, :BLOCK]
            small_ref[16 + groups + g : 17 + groups + g, :] = total[:, BLOCK:]

    return setup, window, finish


def remote(source, target, send, recv, dp, shard):
    return pltpu.make_async_remote_copy(
        src_ref=source,
        dst_ref=target,
        send_sem=send,
        recv_sem=recv,
        device_id={"dp": dp, "shard": shard},
        device_id_type=pl.DeviceIdType.MESH,
    )


def front(
    x_ref,
    key_ref,
    value_ref,
    cot_ref,
    keys_ref,
    values_ref,
    line,
    features,
    panels,
    own,
    outgoing,
    incoming,
    cot_in,
    line_send,
    line_recv,
    plane_send,
    plane_recv,
    core_send,
    core_recv,
    sum_send,
    sum_recv,
    cot_send,
    cot_recv,
    local,
    panel_sem,
    cot_local,
):
    seqs, count, width = x_ref.shape
    blocks, lanes = cot_in.shape[0], cot_in.shape[-1]
    rows = count // PARTS
    chunks = PARTS * seqs
    p, shard = lax.axis_index("dp"), lax.axis_index("shard")
    z, core = shard // 2, shard % 2
    sibling = z * 2 + (1 - core)
    peers = [(p + j) % blocks for j in range(blocks)]
    froms = [(p + blocks - j) % blocks for j in range(blocks)]

    barrier = pltpu.get_barrier_semaphore()

    def greet(dp, to):
        pl.semaphore_signal(
            barrier,
            inc=1,
            device_id={"dp": dp, "shard": to},
            device_id_type=pl.DeviceIdType.MESH,
        )

    greet(p, sibling)
    for j in range(1, blocks):
        greet(peers[j], shard)

    for step in (2, 2 * blocks - 2):
        greet(p, (shard + step) % (2 * blocks))
    pl.semaphore_wait(barrier, blocks + 2)

    def block_of(k):
        return x_ref.at[k // PARTS, pl.ds(k % PARTS * rows, rows)]

    def held(h, layer, k):
        return block_of(k) if h == 0 else line.at[layer, k]

    def line_copy(h, layer, k, way):
        return remote(
            held(h, layer, k),
            line.at[layer, k],
            line_send.at[way, layer, k],
            line_recv.at[layer, k],
            p,
            shard + 2 * (1 - 2 * way),
        )

    def plane_copy(h, layer, k):
        return remote(
            held(h, layer, k),
            features.at[core, k, p],
            plane_send.at[layer, k],
            plane_recv.at[p, k],
            layer,
            shard,
        )

    def plane_arrival(block, k):
        place = features.at[core, k, block]
        return remote(
            place, place, plane_send.at[block, k], plane_recv.at[block, k], block, shard
        )

    def core_copy(source, block, k):
        return remote(
            source,
            features.at[core, k, block],
            core_send.at[block, k],
            core_recv.at[block, k],
            p,
            sibling,
        )

    def core_arrival(block, k):
        place = features.at[1 - core, k, block]
        return remote(place, place, core_send.at[block, k], core_recv.at[block, k], p, sibling)

    def keep_copy(h, layer, k):
        return pltpu.make_async_copy(held(h, layer, k), features.at[core, k, p], local.at[k])

    def steps(h):
        if h == 0:
            return [(0, z, None, z < blocks - 1), (1, z, None, z > 0)]
        return [
            (0, z - h, z - h >= 0, z < blocks - 1),
            (1, z + h, z + h < blocks, z > 0),
        ]

    def dispatch(h, layer, k):
        @pl.when(layer == p)
        def _():
            keep_copy(h, layer, k).start()
            core_copy(held(h, layer, k), p, k).start()

        @pl.when(layer != p)
        def _():
            plane_copy(h, layer, k).start()

    def hop(k, h):
        if h == 0:
            for way, layer, _, onward in steps(0):

                @pl.when(onward)
                def _():
                    line_copy(0, layer, k, way).start()

            dispatch(0, z, k)
            return
        for way, layer, valid, onward in steps(h):

            @pl.when(valid)
            def _():
                line_copy(h, layer, k, way).wait_recv()

                @pl.when(onward)
                def _():
                    line_copy(h, layer, k, way).start()

                dispatch(h, layer, k)

    def share(k):
        for j in range(1, blocks):
            plane_arrival(froms[j], k).wait_recv()
            core_copy(features.at[core, k, froms[j]], froms[j], k).start()

    def complete(k):
        for j in range(blocks):
            core_arrival(froms[j], k).wait_recv()
        keep_copy(0, z, k).wait()

    def sum_copy(k, j):
        return remote(
            outgoing.at[k, j - 1],
            incoming.at[k, j - 1],
            sum_send.at[k, j - 1],
            sum_recv.at[k, j - 1],
            (p + j) % blocks,
            shard,
        )

    def product(k, owner):
        total = jnp.zeros((blocks * rows, 2 * lanes), jnp.float32)
        for c in range(2):
            total += jnp.dot(
                features[c, k].reshape(blocks * rows, width),
                panels[owner, c],
                preferred_element_type=jnp.float32,
            )
        return total

    def project(k):
        def others(j, carry):
            outgoing[k, j - 1] = product(k, (p + j) % blocks).astype(jnp.bfloat16)
            sum_copy(k, j).start()
            return carry

        lax.fori_loop(1, blocks, others, 0)
        own[k] = product(k, p)

    def cot_place(owner):
        return pl.ds(pl.multiple_of(owner * lanes, lanes), lanes)

    def cot_copy(j):
        return remote(
            cot_ref.at[:, :, cot_place(peers[j])],
            cot_in.at[p],
            cot_send.at[j],
            cot_recv.at[p],
            peers[j],
            shard,
        )

    def cot_arrival(j):
        place = cot_in.at[froms[j]]
        return remote(place, place, cot_send.at[j], cot_recv.at[froms[j]], froms[j], shard)

    cot_keep = pltpu.make_async_copy(
        cot_ref.at[:, :, cot_place(p)], cot_in.at[p], cot_local.at[0]
    )
    panel_copies = [
        pltpu.make_async_copy(
            ref.at[pl.ds(c * width, width), pl.ds(r * lanes, lanes)],
            panels.at[r, c, :, pl.ds(branch * lanes, lanes)],
            panel_sem.at[branch, r, c],
        )
        for branch, ref in ((0, key_ref), (1, value_ref))
        for r in range(blocks)
        for c in range(2)
    ]

    def run(prepare):
        hop(0, 0)
        for j in range(1, blocks):
            cot_copy(j).start()
        cot_keep.start()
        for copy in panel_copies:
            copy.start()
        prepare()
        hop(0, 1)
        hop(0, 2)
        hop(1, 0)
        hop(0, 3)
        for k in range(1, chunks):
            hop(k, 1)
            hop(k, 2)
            if k + 1 < chunks:
                hop(k + 1, 0)
            share(k - 1)
            hop(k, 3)
            complete(k - 1)
            if k == 1:
                for copy in panel_copies:
                    copy.wait()
            project(k - 1)
        share(chunks - 1)
        cot_keep.wait()
        for j in range(1, blocks):
            cot_arrival(j).wait_recv()
        complete(chunks - 1)
        project(chunks - 1)

    def collect(w):
        for k in range(PARTS * w, PARTS * (w + 1)):
            for j in range(1, blocks):
                sum_copy(k, j).wait_recv()
            total = own[k]
            for j in range(1, blocks):
                total += incoming[k, j - 1].astype(jnp.float32)
            total = total.astype(jnp.bfloat16).reshape(blocks, rows, 2 * lanes)
            place = pl.ds(k % PARTS * rows, rows)
            keys_ref[k // PARTS, :, place, :] = total[:, :, 0:lanes]
            values_ref[k // PARTS, :, place, :] = total[:, :, lanes : 2 * lanes]

    def drain():
        for k in range(chunks):
            for j in range(1, blocks):
                sum_copy(k, j).wait_send()
            for j in range(blocks):
                core_copy(features.at[core, k, froms[j]], froms[j], k).wait_send()
            for h in range(blocks):
                for way, layer, valid, onward in steps(h):
                    if h > 0:
                        onward = jnp.logical_and(valid, onward)

                    @pl.when(onward)
                    def _():
                        line_copy(h, layer, k, way).wait_send()

                    if h > 0 or way == 0:
                        sent = layer != p
                        if h > 0:
                            sent = jnp.logical_and(valid, sent)

                        @pl.when(sent)
                        def _():
                            plane_copy(h, layer, k).wait_send()

        for j in range(1, blocks):
            cot_copy(j).wait_send()

    return run, collect, drain


def gradients(
    act_ref,
    mixed_ref,
    small_ref,
    mixed_out,
    key_out,
    value_out,
    small_out,
    features,
    turned,
    got,
    mixed_in,
    small_in,
    act_send,
    act_recv,
    mixed_send,
    mixed_recv,
    small_send,
    small_recv,
):
    seqs, blocks, count, both = act_ref.shape
    lanes = both // 2
    width = features.shape[-1]
    p, shard = lax.axis_index("dp"), lax.axis_index("shard")
    x, y = p % 2, p // 2
    beside, above, across = y * 2 + 1 - x, (1 - y) * 2 + x, (1 - y) * 2 + 1 - x
    owners = (p, beside, above, across)

    span = blocks // 2

    def half_of(ref, w, half):
        return ref.at[w, pl.ds(half * span, span)]

    def send_own(slot, w, half):
        return remote(
            half_of(act_ref, w, half),
            half_of(got.at[slot - 1], w, half),
            act_send.at[slot - 1, w, half],
            act_recv.at[slot - 1, w, half],
            owners[slot],
            shard,
        )

    def pass_on(w, half):
        return remote(
            half_of(got.at[half], w, half),
            half_of(got.at[2], w, half),
            act_send.at[2, w, half],
            act_recv.at[2, w, half],
            owners[2 - half],
            shard,
        )

    def arrived(slot, w, half):
        place = half_of(got.at[slot - 1], w, half)
        return remote(
            place,
            place,
            act_send.at[slot - 1, w, half],
            act_recv.at[slot - 1, w, half],
            owners[slot],
            shard,
        )

    def mixed_copy(k):
        return remote(
            mixed_ref.at[owners[k]],
            mixed_in.at[k - 1],
            mixed_send.at[k - 1],
            mixed_recv.at[k - 1],
            owners[k],
            shard,
        )

    def small_copy(k):
        return remote(
            small_ref,
            small_in.at[k - 1],
            small_send.at[k - 1],
            small_recv.at[k - 1],
            owners[k],
            shard,
        )

    def turn(c):
        def tile(i, carry):
            k, block = i // blocks, i % blocks
            rows = count // 2
            begin = ((k // 2 * blocks + block) * 2 + k % 2) * rows
            columns = pl.ds(pl.multiple_of(begin, rows), rows)
            pair = features[c, pl.ds(k * (PARTS // 2), PARTS // 2), block]
            turned[c, :, columns] = pair.reshape(rows, width).T
            return carry

        lax.fori_loop(0, 2 * seqs * blocks, tile, 0)

    def grads(ref, owner):
        place = pl.ds(pl.multiple_of(owner * lanes, lanes), lanes)
        tall = width // 2

        def tile(i, carry):
            c, half = i // 2, i % 2
            rows = pl.ds(pl.multiple_of(half * tall, tall), tall)
            total = jnp.dot(
                turned[c, rows, :],
                ref[...].reshape(seqs * blocks * count, both),
                preferred_element_type=jnp.float32,
            ).astype(jnp.bfloat16)
            out = pl.ds(pl.multiple_of(i * tall, tall), tall)
            key_out[out, place] = total[:, :lanes]
            value_out[out, place] = total[:, lanes:]
            return carry

        lax.fori_loop(0, 4, tile, 0)

    def send(w):
        for slot, half in ((1, 0), (2, 1), (1, 1), (2, 0)):
            send_own(slot, w, half).start()

    def forward(w):
        for half in range(2):
            arrived(1 + half, w, half).wait_recv()
            pass_on(w, half).start()

    def spread():
        for k in range(1, blocks):
            mixed_copy(k).start()
            small_copy(k).start()

    def run():
        forward(0)
        turn(0)
        forward(1)
        turn(1)
        grads(act_ref, p)
        for slot, owner in ((1, beside), (2, above)):
            for w in range(seqs):
                arrived(slot, w, 2 - slot).wait_recv()
            grads(got.at[slot - 1], owner)
        small_out[p] = small_ref[...]
        for k in range(1, blocks):
            small_copy(k).wait_recv()
            small_out[owners[k]] = small_in[k - 1]
        mixed_out[:, :, pl.ds(pl.multiple_of(p * lanes, lanes), lanes)] = mixed_ref[p]
        for k in range(1, blocks):
            mixed_copy(k).wait_recv()
            place = pl.ds(pl.multiple_of(owners[k] * lanes, lanes), lanes)
            mixed_out[:, :, place] = mixed_in[k - 1]
        for w in range(seqs):
            for half in range(2):
                arrived(3, w, half).wait_recv()
        grads(got.at[2], across)
        for w in range(seqs):
            for half in range(2):
                send_own(1, w, half).wait_send()
                send_own(2, w, half).wait_send()
                pass_on(w, half).wait_send()
        for k in range(1, blocks):
            mixed_copy(k).wait_send()
            small_copy(k).wait_send()

    return send, forward, spread, run


def operator_kernel(taps, group, *refs):
    (x_ref, key_ref, value_ref, cot_ref, lengths_ref, short_ref, medium_ref, reversed_ref) = refs[:8]
    outs, keys_ref, values_ref = refs[8:12], refs[12], refs[13]
    act_ref, mixed_ref, small_ref = refs[14:17]
    front_refs, filter_refs, back_refs = refs[17:37], refs[37:46], refs[46:]
    features, cot_in = front_refs[1], front_refs[6]
    project, collect, drain = front(
        x_ref, key_ref, value_ref, cot_ref, keys_ref, values_ref, *front_refs
    )
    setup, window, finish = filters(
        taps,
        group,
        lengths_ref,
        keys_ref,
        values_ref,
        cot_in,
        short_ref,
        medium_ref,
        reversed_ref,
        mixed_ref,
        act_ref,
        small_ref,
        *filter_refs,
    )
    send, forward, spread, run = gradients(
        act_ref, mixed_ref, small_ref, *outs, features, *back_refs
    )
    project(setup)
    for w in range(keys_ref.shape[0]):
        collect(w)
        window(w)
        send(w)
    finish()
    spread()
    run()
    drain()


def operator(inputs, key_panel, value_panel, cotangent, lengths, short_filters, medium_filters, blocks):
    seqs, count, width = inputs.shape
    channels = key_panel.shape[1]
    lanes = channels // blocks
    groups, medium = medium_filters.shape
    taps = short_filters.shape[-1]
    length = blocks * count
    short = jnp.pad(short_filters.transpose(0, 2, 1), ((0, 0), (0, 8 - taps), (0, 0)))
    ahead = jnp.pad(medium_filters, ((0, 0), (0, 2 * BLOCK - medium)))
    behind = jnp.pad(medium_filters[:, ::-1], ((0, 0), (BLOCK + 1 - medium, BLOCK - 1)))
    pieces = PARTS * seqs
    tall = blocks * count // PARTS
    vmem = pl.BlockSpec(memory_space=pltpu.VMEM)
    hbm = pl.BlockSpec(memory_space=pl.ANY)
    dma = pltpu.SemaphoreType.DMA
    small_shape = (16 + 2 * groups, lanes)
    act_shape = (seqs, blocks, count, 2 * lanes)
    panel = jax.ShapeDtypeStruct((2 * width, channels), jnp.bfloat16)
    return pl.pallas_call(
        functools.partial(operator_kernel, taps, lanes // groups),
        out_shape=(
            jax.ShapeDtypeStruct((seqs, count, channels), jnp.bfloat16),
            panel,
            panel,
            jax.ShapeDtypeStruct((blocks,) + small_shape, jnp.float32),
        ),
        in_specs=[hbm] * 4 + [pl.BlockSpec(memory_space=pltpu.SMEM)] + [vmem] * 3,
        out_specs=[vmem] * 4,
        scratch_shapes=[
            pltpu.VMEM((seqs, blocks, count, lanes), jnp.bfloat16),
            pltpu.VMEM((seqs, blocks, count, lanes), jnp.bfloat16),
            pltpu.VMEM(act_shape, jnp.bfloat16),
            pltpu.VMEM((blocks, seqs, count, lanes), jnp.bfloat16),
            pltpu.VMEM(small_shape, jnp.float32),
            pltpu.VMEM((blocks, pieces, count // PARTS, width), jnp.bfloat16),
            pltpu.VMEM((2, pieces, blocks, count // PARTS, width), jnp.bfloat16),
            pltpu.VMEM((blocks, 2, width, 2 * lanes), jnp.bfloat16),
            pltpu.VMEM((pieces, tall, 2 * lanes), jnp.float32),
            pltpu.VMEM((pieces, blocks - 1, tall, 2 * lanes), jnp.bfloat16),
            pltpu.VMEM((pieces, blocks - 1, tall, 2 * lanes), jnp.bfloat16),
            pltpu.VMEM((blocks, seqs, count, lanes), jnp.bfloat16),
            dma((2, blocks, pieces)),
            dma((blocks, pieces)),
            dma((blocks, pieces)),
            dma((blocks, pieces)),
            dma((blocks, pieces)),
            dma((blocks, pieces)),
            dma((pieces, blocks - 1)),
            dma((pieces, blocks - 1)),
            dma((blocks,)),
            dma((blocks,)),
        ]
        + [dma((pieces,)), dma((2, blocks, 2)), dma((1,))]
        + [
            pltpu.VMEM((2, seqs, length + 8, lanes), jnp.float32),
            pltpu.VMEM((2, seqs, length, lanes), jnp.float32),
            pltpu.VMEM((2, seqs, length + 8, lanes), jnp.float32),
            pltpu.VMEM((length + BLOCK, seqs * lanes), jnp.bfloat16),
            pltpu.VMEM((length + BLOCK, seqs * lanes), jnp.bfloat16),
            pltpu.VMEM((groups * BLOCK, 2 * BLOCK), jnp.bfloat16),
            pltpu.VMEM((groups * BLOCK, 2 * BLOCK), jnp.bfloat16),
            pltpu.VMEM((groups * BLOCK, 2 * BLOCK), jnp.float32),
            pltpu.VMEM((2, taps, 8, lanes), jnp.float32),
            pltpu.VMEM((2, width, seqs * blocks * count), jnp.bfloat16),
            pltpu.VMEM((3,) + act_shape, jnp.bfloat16),
            pltpu.VMEM((blocks - 1, seqs, count, lanes), jnp.bfloat16),
            pltpu.VMEM((blocks - 1,) + small_shape, jnp.float32),
            dma((3, seqs, 2)),
            dma((3, seqs, 2)),
            dma((blocks - 1,)),
            dma((blocks - 1,)),
            dma((blocks - 1,)),
            dma((blocks - 1,)),
        ],
        compiler_params=pltpu.CompilerParams(
            collective_id=0, has_side_effects=True, vmem_limit_bytes=62 * 1024 * 1024
        ),
        cost_estimate=pl.CostEstimate(
            flops=8 * blocks * seqs * count * 2 * width * channels,
            bytes_accessed=8 * blocks * seqs * count * width,
            transcendentals=0,
        ),
    )(inputs, key_panel, value_panel, cotangent, lengths, short, ahead, behind)


def by_channels(inputs, key_panel, value_panel, short_filters, medium_filters, lengths, cotangent):
    blocks = lax.axis_size("dp")
    channels = key_panel.shape[1]
    lanes = channels // blocks
    groups = medium_filters.shape[0] // blocks
    mine = lax.axis_index("dp")
    short = lax.dynamic_slice_in_dim(short_filters, mine * lanes, lanes, 1)
    medium = lax.dynamic_slice_in_dim(medium_filters, mine * groups, groups, 0)
    mixed, key_grad, value_grad, small = operator(
        inputs, key_panel, value_panel, cotangent, lengths, short, medium, blocks
    )
    taps, medium_taps = short_filters.shape[-1], medium_filters.shape[-1]
    short_grad = small[:, :16].reshape(blocks, 2, 8, lanes)[:, :, :taps]
    short_grad = short_grad.transpose(1, 0, 3, 2).reshape(2, channels, taps)
    sums = small[:, 16:].reshape(blocks, 2, groups, BLOCK).transpose(0, 2, 1, 3)
    sums = sums.reshape(blocks * groups, 2 * BLOCK)
    medium_grad = sums[:, BLOCK - medium_taps + 1 : BLOCK + 1][:, ::-1]
    return (mixed, key_grad, value_grad, short_grad, medium_grad)


def shards(inputs, key_panel, value_panel, short_filters, medium_filters, lengths, cotangent):
    blocks, shard = lax.axis_size("dp"), lax.axis_size("shard")
    channels = key_panel.shape[1]
    whole = channels == blocks * BLOCK and inputs.shape[1] % (2 * BLOCK) == 0
    plan = by_channels if whole and blocks == 4 and shard == 2 * blocks else by_positions
    return plan(
        inputs, key_panel, value_panel, short_filters, medium_filters, lengths, cotangent
    )


def solution(mesh):
    return jax.shard_map(
        shards,
        mesh=mesh,
        in_specs=(
            P(None, "dp", "shard"),
            P("dp", "shard"),
            P("dp", "shard"),
            P(None, "shard", None),
            P("shard", None),
            P(),
            P(None, "dp", "shard"),
        ),
        out_specs=(
            P(None, "dp", "shard"),
            P("dp", "shard"),
            P("dp", "shard"),
            P(None, "shard", None),
            P("shard", None),
        ),
        check_vma=False,
    )
```
